256 devices in a mesh: dp: 4 (over x), row: 4 (over z_lo), col: 16 (over y, z_hi, core).
Axes of the slice: x: 4, y: 4, z: 8 (z_hi: 2, z_lo: 4; z = z_hi * 4 + z_lo), core: 2. Of those that a mesh axis runs over, the one named last changes fastest.
Arguments:
- inputs: bfloat16 [2048, 8192], P(('dp', 'row'), 'col'), may hold values from -64 to 64
- grad_out: bfloat16 [2048, 4, 8192], P(('dp', 'col'), None, 'row')
- row_moment: float32 [8192], P('col'), may hold values from 0.01 to 1.5
- column_moment: float32 [32768], P(('dp', 'row')), may hold values from 0.05 to 0.5
Outputs:
- update: float32 [8192, 32768], P('col', ('dp', 'row'))
- row_state: float32 [8192], P('col')
- column_state: float32 [32768], P(('dp', 'row'))
- row_mean: float32 [], replicated
The draws below stay inside these ranges and needn't reach their ends.
All inputs are finite; a program needn't handle non-finite values.
Results may differ from the reference program's by a relative error of at most 0.0004.
Values may be sent and summed in bfloat16 or wider, within the bound.
No kernel may reach another device: no remote copies, remote signals or barrier semaphores. Data moves between devices by JAX's collectives and lax.ppermute only.
A program may use at most 128 MiB of HBM per device.

```python
import math
import jax
import jax.numpy as jnp
from jax import lax

D = 8192
FF = 32768
BLOCKS = 4
TOKENS = 2048


def column_scales(key, amount):
    rough = jnp.exp(jax.random.uniform(key, (amount,), minval=-1.15, maxval=1.15))
    ramp = jnp.exp(jnp.log(3.0) * (jnp.arange(amount, dtype=jnp.float32) / amount - 0.5))
    return rough * ramp


def draw_inputs(key, part):
    key = jax.random.fold_in(key, 11)
    first, second = jax.random.split(key, 2)
    scales = column_scales(first, D)
    values = jax.random.normal(second, (TOKENS, D))
    return (values * scales[None, :]).astype(jnp.bfloat16)


def draw_grad_out(key, part):
    key = jax.random.fold_in(key, 23)
    first, second = jax.random.split(key, 2)
    scales = column_scales(first, FF).reshape(BLOCKS, FF // BLOCKS)
    values = jax.random.normal(second, (TOKENS, BLOCKS, FF // BLOCKS))
    return (values * scales[None, :, :] * TOKENS ** (-0.5)).astype(jnp.bfloat16)


def rising_factor(key, amount, spread):
    rough = jnp.exp(jax.random.uniform(key, (amount,), minval=-1.0, maxval=1.0))
    ramp = jnp.exp(jnp.log(spread) * (jnp.arange(amount, dtype=jnp.float32) / amount - 0.5))
    return 0.15 * rough * ramp


def draw_row_moment(key, part):
    key = jax.random.fold_in(key, 37)
    values = rising_factor(key, D, 3.0)
    return values.astype(jnp.float32)


def level_of(key, dims, pieces, least, largest):
    def one(dim, shards_of):
        heights = jax.random.uniform(jax.random.fold_in(jax.random.fold_in(key, 6), dim), (shards_of,), jnp.float32, least / len(pieces), largest / len(pieces))
        return jnp.repeat(jnp.exp(heights), dims[dim] // shards_of).reshape((-1,) + (1,) * (len(dims) - dim - 1))

    level = one(*pieces[0])
    for cut in pieces[1:]:
        level = level * one(*cut)
    return level


def setup_inputs(seed: int = 0) -> dict:
    splits = jax.random.split(jax.random.key(seed), 5)
    return {
        "inputs": draw_inputs(jax.random.fold_in(splits[4], 71), 0),
        "grad_out": draw_grad_out(jax.random.fold_in(splits[4], 71), 0),
        "row_moment": draw_row_moment(jax.random.fold_in(splits[4], 71), 0),
        "column_moment": jnp.clip(jnp.exp(math.log(0.5) - 2.3025851 * jax.random.uniform(splits[3], (FF,), jnp.float32) ** level_of(splits[3], (FF,), ((0, 16),), -0.2, 0.2)), 0.05, 0.5),
    }


def reference(inputs, grad_out, row_moment, column_moment):
    flattened = grad_out.reshape(grad_out.shape[0], -1)
    gradient = lax.dot_general(inputs, flattened, (((0,), (0,)), ((), ())), preferred_element_type=jnp.float32)
    squares = gradient * gradient + 1e-30
    row_state = 0.8 * row_moment + 0.2 * lax.optimization_barrier(jnp.sum(squares, axis=1)) / FF
    column_state = 0.8 * column_moment + 0.2 * lax.optimization_barrier(jnp.sum(squares, axis=0)) / D
    row_mean = jnp.sum(row_state) / D
    scaled_step = gradient / jnp.sqrt(row_state[:, None] * column_state[None, :] / row_mean)
    clip_ratio = jnp.sqrt(jnp.sum(scaled_step * scaled_step) / (D * FF))
    update = scaled_step / jnp.maximum(1.0, clip_ratio)
    return (update, row_state, column_state, row_mean)
```

```python
import jax
import jax.numpy as jnp
from jax import lax
from jax.experimental import pallas as pl
from jax.experimental.pallas import tpu as pltpu
from jax.sharding import PartitionSpec as P

D = 8192
FF = 32768
VMEM_LIMIT = 40 * 1024 * 1024
COLS = 512


def arrange_kernel(at_ref, x0_ref, x1_ref, x2a_ref, x2b_ref, x3_ref, near_ref, far_ref, x2_ref):
    half = x2a_ref.shape[0]
    x2_ref[0:half, :] = x2a_ref[...]
    x2_ref[half:, :] = x2b_ref[...]
    pieces = (x0_ref, x1_ref, x2_ref, x3_ref)
    for far, out_ref in ((0, near_ref), (1, far_ref)):
        for other in (0, 1):
            for t in range(4):
                start = at_ref[t] + at_ref[4 + far] + at_ref[6 + other]
                start = pl.multiple_of(start, 32)
                rows = [piece[pl.ds(start, 32), :] for piece in pieces]
                block = jnp.concatenate(rows, axis=0).T
                column = other * 512 + t * 128
                out_ref[:, column : column + 128] = block


def arrange(at, pieces):
    whole = pl.BlockSpec(memory_space=pltpu.VMEM)
    return pl.pallas_call(
        arrange_kernel,
        in_specs=[pl.BlockSpec(memory_space=pltpu.SMEM)] + [whole] * 5,
        out_specs=[whole] * 2,
        out_shape=[jax.ShapeDtypeStruct((512, 1024), jnp.bfloat16)] * 2,
        scratch_shapes=[pltpu.VMEM((512, 512), jnp.bfloat16)],
        compiler_params=pltpu.CompilerParams(vmem_limit_bytes=VMEM_LIMIT),
        cost_estimate=pl.CostEstimate(flops=0, bytes_accessed=4 << 20, transcendentals=0),
    )(at, *pieces)


def both(x_ref, own_ref, other_ref):
    return jnp.dot(
        x_ref[:, 0:512], own_ref[...], preferred_element_type=jnp.float32
    ) + jnp.dot(x_ref[:, 512:1024], other_ref[...], preferred_element_type=jnp.float32)


def near_kernel(x_ref, own_ref, other_ref, out_ref):
    out_ref[...] = both(x_ref, own_ref, other_ref)


def far_kernel(x_ref, own_ref, other_ref, near_ref, out_ref, col_ref, row_ref, acc_ref):
    step = pl.program_id(0)
    value = near_ref[...] + both(x_ref, own_ref, other_ref)
    out_ref[...] = value
    squares = value * value + 1e-30
    col_ref[...] = jnp.sum(squares, axis=0, keepdims=True)
    part = squares[:, 0:128]
    for k in range(1, COLS // 128):
        part = part + squares[:, k * 128 : (k + 1) * 128]

    @pl.when(step == 0)
    def _():
        acc_ref[...] = part

    @pl.when(step > 0)
    def _():
        acc_ref[...] += part

    @pl.when(step == pl.num_programs(0) - 1)
    def _():
        row_ref[...] = jnp.sum(acc_ref[...].T, axis=0, keepdims=True)


X_SPEC = pl.BlockSpec((512, 1024), lambda j: (0, 0))
G_SPEC = pl.BlockSpec((512, COLS), lambda j: (0, j))
PARAMS = pltpu.CompilerParams(vmem_limit_bytes=VMEM_LIMIT)
COST = pl.CostEstimate(flops=2 * 512 * 1024 * 2048, bytes_accessed=9 << 20, transcendentals=0)


def near_product(x, own, other):
    return pl.pallas_call(
        near_kernel,
        grid=(2048 // COLS,),
        in_specs=[X_SPEC, G_SPEC, G_SPEC],
        out_specs=G_SPEC,
        out_shape=jax.ShapeDtypeStruct((512, 2048), jnp.float32),
        compiler_params=PARAMS,
        cost_estimate=COST,
    )(x, own, other)


def far_product(x, own, other, near):
    return pl.pallas_call(
        far_kernel,
        grid=(2048 // COLS,),
        in_specs=[X_SPEC, G_SPEC, G_SPEC, G_SPEC],
        out_specs=[
            G_SPEC,
            pl.BlockSpec((1, COLS), lambda j: (0, j)),
            pl.BlockSpec((1, 512), lambda j: (0, 0)),
        ],
        out_shape=[
            jax.ShapeDtypeStruct((512, 2048), jnp.float32),
            jax.ShapeDtypeStruct((1, 2048), jnp.float32),
            jax.ShapeDtypeStruct((1, 512), jnp.float32),
        ],
        scratch_shapes=[pltpu.VMEM((512, 128), jnp.float32)],
        compiler_params=PARAMS,
        cost_estimate=COST,
    )(x, own, other, near)


def scale_kernel(g_ref, row_ref, col_ref, out_ref, total_ref, acc_ref, rows_ref):
    step = pl.program_id(0)

    @pl.when(step == 0)
    def _():
        rows_ref[...] = jnp.broadcast_to(lax.rsqrt(row_ref[...]), (128, row_ref.shape[1])).T

    v = lax.rsqrt(col_ref[...])
    u = rows_ref[...]
    part = jnp.zeros(u.shape, jnp.float32)
    for k in range(COLS // 128):
        piece = slice(k * 128, (k + 1) * 128)
        scaled = g_ref[:, piece] * u * v[:, piece]
        out_ref[:, piece] = scaled
        part = part + scaled * scaled

    @pl.when(step == 0)
    def _():
        acc_ref[...] = part

    @pl.when(step > 0)
    def _():
        acc_ref[...] += part

    @pl.when(step == pl.num_programs(0) - 1)
    def _():
        total = jnp.sum(acc_ref[...])
        states = jnp.sum(row_ref[...])
        lane = lax.broadcasted_iota(jnp.int32, (1, 128), 1)
        total_ref[...] = jnp.where(lane == 0, total, jnp.where(lane == 1, states, 0.0))


def scale(g, row_state, column_state):
    rows, units = g.shape
    return pl.pallas_call(
        scale_kernel,
        grid=(units // COLS,),
        in_specs=[
            pl.BlockSpec((rows, COLS), lambda j: (0, j)),
            pl.BlockSpec((1, rows), lambda j: (0, 0)),
            pl.BlockSpec((1, COLS), lambda j: (0, j)),
        ],
        out_specs=[
            pl.BlockSpec((rows, COLS), lambda j: (0, j)),
            pl.BlockSpec((1, 128), lambda j: (0, 0)),
        ],
        out_shape=[
            jax.ShapeDtypeStruct((rows, units), jnp.float32),
            jax.ShapeDtypeStruct((1, 128), jnp.float32),
        ],
        scratch_shapes=[
            pltpu.VMEM((rows, 128), jnp.float32),
            pltpu.VMEM((rows, 128), jnp.float32),
        ],
        compiler_params=pltpu.CompilerParams(vmem_limit_bytes=VMEM_LIMIT),
        cost_estimate=pl.CostEstimate(
            flops=5 * rows * units, bytes_accessed=8 << 20, transcendentals=0
        ),
    )(g, row_state, column_state)


def cyclic(size, stride, shift):
    total = size * stride
    return [(j, (j + shift * stride) % total) for j in range(total)]


def flipped(total, mask):
    return [(j, j ^ mask) for j in range(total)]


def sum_of_four(value, axis, perms):
    a, b, c = [lax.ppermute(value, axis, perm) for perm in perms]
    return (value + a) + (b + c)


RING = [cyclic(4, 1, 2), cyclic(4, 1, 1), cyclic(4, 1, 3)]
Y_RING = [cyclic(4, 4, 2), cyclic(4, 4, 1), cyclic(4, 4, 3)]
PAIRS = [flipped(16, 1), flipped(16, 2), flipped(16, 3)]


def over_col(value):
    return sum_of_four(sum_of_four(value, "col", Y_RING), "col", PAIRS)


def over_dp_row(value):
    return sum_of_four(sum_of_four(value, "dp", RING), "row", RING)


def along_z(shift):
    pairs = []
    for j in range(64):
        low, y, high, core = j // 16, j // 4 % 4, j // 2 % 2, j % 2
        z = (high * 4 + low + shift) % 8
        pairs.append((j, z % 4 * 16 + y * 4 + z // 4 * 2 + core))
    return pairs


UP = cyclic(4, 4, 1)
DOWN = cyclic(4, 4, 3)


def over_y(block):
    one = lax.ppermute(block, "col", UP)
    three = lax.ppermute(block, "col", DOWN)
    two_a = lax.ppermute(one[0:64], "col", UP)
    two_b = lax.ppermute(three[64:128], "col", DOWN)
    own = jnp.concatenate([block, one, two_a, two_b, three])
    return own, lax.ppermute(own, "col", flipped(16, 1))


def per_device(inputs, grad_out, row_moment, column_moment):
    me = lax.axis_index("dp")
    low = lax.axis_index("row")
    col = lax.axis_index("col")
    y, high, core = col // 4, col // 2 % 2, col % 2
    by_group = jnp.transpose(grad_out, (1, 0, 2))

    def group(g):
        return lax.dynamic_index_in_dim(by_group, g, 0, keepdims=False)

    blocks = [group(me)]
    for s in (1, 2, 3):
        blocks.append(lax.ppermute(group((me + s) % 4), "dp", cyclic(4, 1, s)))
    near = jnp.concatenate(blocks)

    rows = [inputs] + [lax.ppermute(inputs, "row", cyclic(4, 1, t)) for t in (1, 2, 3)]
    x0 = jnp.concatenate(rows)
    x1 = lax.ppermute(x0, "dp", cyclic(4, 1, 1))
    x3 = lax.ppermute(x0, "dp", cyclic(4, 1, 3))
    x2a = lax.ppermute(x1[0:256], "dp", cyclic(4, 1, 1))
    x2b = lax.ppermute(x3[256:512], "dp", cyclic(4, 1, 3))

    far_a = lax.ppermute(near[0:64], "col", flipped(16, 2))
    halfway = lax.ppermute(near[64:128], ("row", "col"), along_z(-2))
    far_b = lax.ppermute(halfway, ("row", "col"), along_z(-2))
    far = jnp.concatenate([far_a, far_b])

    starts = [(low - (y - t)) % 4 * 128 for t in range(4)]
    starts += [high * 64, (1 - high) * 64, core * 32, (1 - core) * 32]
    at = jnp.stack(starts).astype(jnp.int32)
    x_near, x_far = arrange(at, (x0, x1, x2a, x2b, x3))

    gradient = near_product(x_near, *over_y(near))
    gradient, column_part, row_part = far_product(x_far, *over_y(far), gradient)

    column_sums = over_col(column_part)
    row_sums = over_dp_row(row_part)
    row_state = 0.8 * row_moment[None] + 0.2 * row_sums / FF
    column_state = 0.8 * column_moment[None] + 0.2 * column_sums / D
    scaled, totals = scale(gradient, row_state, column_state)
    totals = over_dp_row(over_col(totals))
    row_mean = totals[0, 1] / (16 * D)
    clip_ratio = jnp.sqrt(row_mean * totals[0, 0] / (D * FF))
    update = scaled * (jnp.sqrt(row_mean) / jnp.maximum(1.0, clip_ratio))
    return (update, row_state[0], column_state[0], row_mean)


def solution(mesh):
    return jax.shard_map(
        per_device,
        mesh=mesh,
        in_specs=(
            P(("dp", "row"), "col"),
            P(("dp", "col"), None, "row"),
            P("col"),
            P(("dp", "row")),
        ),
        out_specs=(P("col", ("dp", "row")), P("col"), P(("dp", "row")), P()),
        check_vma=False,
    )
```

```python
import jax
import jax.numpy as jnp
from jax import lax
from jax.experimental import pallas as pl
from jax.experimental.pallas import tpu as pltpu
from jax.sharding import PartitionSpec as P

D = 8192
FF = 32768
VMEM_LIMIT = 24 * 1024 * 1024
COLS = 512
ORDER = [(s, t) for t in (0, 1, 3, 2) for s in range(4)]


def arrange_kernel(at_ref, x0_ref, x1_ref, x2a_ref, x2b_ref, x3_ref, near_ref, far_ref, x2_ref):
    half = x2a_ref.shape[0]
    x2_ref[0:half, :] = x2a_ref[...]
    x2_ref[half:, :] = x2b_ref[...]
    pieces = (x0_ref, x1_ref, x2_ref, x3_ref)

    def put(out_ref, column, offset, blocks):
        rows = []
        for s, t in blocks:
            start = pl.multiple_of(at_ref[t] + offset, 32)
            rows.append(pieces[s][pl.ds(start, 32), :])
        out_ref[:, column : column + 128] = jnp.concatenate(rows, axis=0).T

    for other in (0, 1):
        near = at_ref[4] + at_ref[6 + other]
        far = at_ref[5] + at_ref[6 + other]
        for k in range(4):
            blocks = ORDER[4 * k : 4 * k + 4]
            put(near_ref, other * 512 + k * 128, near, blocks)
            put(far_ref, other * 512 + k * 128, far, blocks)


def arrange(at, pieces):
    whole = pl.BlockSpec(memory_space=pltpu.VMEM)
    return pl.pallas_call(
        arrange_kernel,
        in_specs=[pl.BlockSpec(memory_space=pltpu.SMEM)] + [whole] * 5,
        out_specs=[whole] * 2,
        out_shape=[jax.ShapeDtypeStruct((512, 1024), jnp.bfloat16)] * 2,
        scratch_shapes=[pltpu.VMEM((512, 512), jnp.bfloat16)],
        compiler_params=PARAMS,
        cost_estimate=pl.CostEstimate(flops=0, bytes_accessed=4 << 20, transcendentals=0),
    )(at, *pieces)


def near_kernel(x_ref, own_ref, other_ref, out_ref):
    out_ref[...] = jnp.dot(
        x_ref[:, 0:512], own_ref[...], preferred_element_type=jnp.float32
    ) + jnp.dot(x_ref[:, 512:1024], other_ref[...], preferred_element_type=jnp.float32)


def across(value):
    part = value[:, 0:128]
    for k in range(1, COLS // 128):
        part = part + value[:, k * 128 : (k + 1) * 128]
    return part


def gather_rows(step, part, acc_ref, row_ref):
    @pl.when(step == 0)
    def _():
        acc_ref[...] = part

    @pl.when(step > 0)
    def _():
        acc_ref[...] += part

    @pl.when(step == pl.num_programs(0) - 1)
    def _():
        row_ref[...] = jnp.sum(acc_ref[...].T, axis=0, keepdims=True)


def far_kernel(
    x_ref, own_ref, own_last_ref, other_ref, other_last_ref, near_ref,
    out_ref, col_ref, row_ref, acc_ref,
):
    value = near_ref[...]
    own = jnp.concatenate([own_ref[...], own_last_ref[...]], axis=0)
    value += jnp.dot(x_ref[:, 0:512], own, preferred_element_type=jnp.float32)
    other = jnp.concatenate([other_ref[...], other_last_ref[...]], axis=0)
    value += jnp.dot(x_ref[:, 512:1024], other, preferred_element_type=jnp.float32)
    out_ref[...] = value
    squares = value * value + 1e-30
    col_ref[...] = jnp.sum(squares, axis=0, keepdims=True)
    gather_rows(pl.program_id(0), across(squares), acc_ref, row_ref)


def fixed(*shape):
    return pl.BlockSpec(shape, lambda j: (0, 0))


def moving(rows):
    return pl.BlockSpec((rows, COLS), lambda j: (0, j))


G_SPEC = moving(512)
PARAMS = pltpu.CompilerParams(vmem_limit_bytes=VMEM_LIMIT)
COST = pl.CostEstimate(flops=2 * 512 * 1024 * 2048, bytes_accessed=9 << 20, transcendentals=0)


def near_product(x, own, other):
    return pl.pallas_call(
        near_kernel,
        grid=(2048 // COLS,),
        in_specs=[fixed(512, 1024), moving(512), moving(512)],
        out_specs=G_SPEC,
        out_shape=jax.ShapeDtypeStruct((512, 2048), jnp.float32),
        compiler_params=PARAMS,
        cost_estimate=COST,
    )(x, own, other)


def far_product(x, own, own_last, other, other_last, near):
    return pl.pallas_call(
        far_kernel,
        grid=(2048 // COLS,),
        in_specs=[fixed(512, 1024), moving(384), moving(128), moving(384), moving(128), G_SPEC],
        out_specs=[G_SPEC, moving(1), fixed(1, 512)],
        out_shape=[
            jax.ShapeDtypeStruct((512, 2048), jnp.float32),
            jax.ShapeDtypeStruct((1, 2048), jnp.float32),
            jax.ShapeDtypeStruct((1, 512), jnp.float32),
        ],
        scratch_shapes=[pltpu.VMEM((512, 128), jnp.float32)],
        compiler_params=PARAMS,
        cost_estimate=COST,
    )(x, own, own_last, other, other_last, near)


def weigh_kernel(g_ref, moment_ref, sums_ref, row_ref, state_ref, out_ref, acc_ref, weighed_ref):
    step = pl.program_id(0)
    state = 0.8 * moment_ref[...] + 0.2 * sums_ref[...] / D
    state_ref[...] = state
    scaled = g_ref[...] * lax.rsqrt(state)
    gather_rows(step, across(scaled * scaled), acc_ref, weighed_ref)

    @pl.when(step == pl.num_programs(0) - 1)
    def _():
        out_ref[0:1, :] = row_ref[...]
        out_ref[1:2, :] = weighed_ref[...]


def weigh(g, column_moment, column_sums, row_part):
    return pl.pallas_call(
        weigh_kernel,
        grid=(2048 // COLS,),
        in_specs=[G_SPEC, moving(1), moving(1), fixed(1, 512)],
        out_specs=[moving(1), fixed(2, 512)],
        out_shape=[
            jax.ShapeDtypeStruct((1, 2048), jnp.float32),
            jax.ShapeDtypeStruct((2, 512), jnp.float32),
        ],
        scratch_shapes=[
            pltpu.VMEM((512, 128), jnp.float32),
            pltpu.VMEM((1, 512), jnp.float32),
        ],
        compiler_params=PARAMS,
        cost_estimate=pl.CostEstimate(
            flops=4 * 512 * 2048, bytes_accessed=4 << 20, transcendentals=0
        ),
    )(g, column_moment, column_sums, row_part)


def totals_kernel(moment_ref, sums_ref, state_ref, total_ref):
    state = 0.8 * moment_ref[...] + 0.2 * sums_ref[0:1, :] / FF
    state_ref[...] = state
    squares = jnp.sum(sums_ref[1:2, :] / state)
    lane = lax.broadcasted_iota(jnp.int32, (1, 128), 1)
    total_ref[...] = jnp.where(lane == 0, squares, jnp.where(lane == 1, jnp.sum(state), 0.0))


def totals_of(row_moment, sums):
    return pl.pallas_call(
        totals_kernel,
        out_shape=[
            jax.ShapeDtypeStruct((1, 512), jnp.float32),
            jax.ShapeDtypeStruct((1, 128), jnp.float32),
        ],
        compiler_params=PARAMS,
        cost_estimate=pl.CostEstimate(flops=2048, bytes_accessed=8192, transcendentals=0),
    )(row_moment, sums)


def clip_kernel(g_ref, row_ref, col_ref, totals_ref, out_ref, mean_ref, rows_ref):
    @pl.when(pl.program_id(0) == 0)
    def _():
        rows_ref[...] = jnp.broadcast_to(lax.rsqrt(row_ref[...]), (128, 512)).T

    lane = lax.broadcasted_iota(jnp.int32, (1, 128), 1)
    totals = totals_ref[...]
    total = jnp.sum(jnp.where(lane == 0, totals, 0.0), axis=1, keepdims=True)
    row_mean = jnp.sum(jnp.where(lane == 1, totals, 0.0), axis=1, keepdims=True) / D
    mean_ref[...] = row_mean
    clip_ratio = jnp.sqrt(row_mean * total / (D * FF))
    factor = jnp.sqrt(row_mean) / jnp.maximum(1.0, clip_ratio)
    columns = lax.rsqrt(col_ref[...]) * factor
    rows = rows_ref[...]
    for k in range(COLS // 128):
        piece = slice(k * 128, (k + 1) * 128)
        out_ref[:, piece] = g_ref[:, piece] * rows * columns[:, piece]


def clip(g, row_state, column_state, totals):
    return pl.pallas_call(
        clip_kernel,
        grid=(2048 // COLS,),
        in_specs=[G_SPEC, fixed(1, 512), moving(1), fixed(1, 128)],
        out_specs=[G_SPEC, fixed(1, 1)],
        out_shape=[
            jax.ShapeDtypeStruct((512, 2048), jnp.float32),
            jax.ShapeDtypeStruct((1, 1), jnp.float32),
        ],
        scratch_shapes=[pltpu.VMEM((512, 128), jnp.float32)],
        compiler_params=PARAMS,
        cost_estimate=pl.CostEstimate(
            flops=2 * 512 * 2048, bytes_accessed=8 << 20, transcendentals=0
        ),
    )(g, row_state, column_state, totals)


def cyclic(size, stride, shift):
    total = size * stride
    return [(j, (j + shift * stride) % total) for j in range(total)]


def flipped(total, mask):
    return [(j, j ^ mask) for j in range(total)]


def swap_cores(value):
    return lax.ppermute(value, "col", flipped(16, 1))


def move_x(value, shift):
    return lax.ppermute(value, "dp", cyclic(4, 1, shift % 4))


def move_y(value, shift):
    return lax.ppermute(value, "col", cyclic(4, 4, shift % 4))


def swap_row(value, mask):
    return lax.ppermute(value, "row", flipped(4, mask))


def swap_z(value):
    return lax.ppermute(value, "col", flipped(16, 2))


def over(value, axis, masks):
    size = 16 if axis == "col" else 4
    for mask in masks:
        value = value + lax.ppermute(value, axis, flipped(size, mask))
    return value


def over_col(value):
    return over(value, "col", (1, 4, 8, 2))


def over_dp_row(value):
    return over(over(value, "dp", (1, 2)), "row", (1, 2))


def per_device(inputs, grad_out, row_moment, column_moment):
    me = lax.axis_index("dp")
    low = lax.axis_index("row")
    col = lax.axis_index("col")
    y, high, core = col // 4, col // 2 % 2, col % 2
    starts = [(low ^ ((y - t) % 4)) * 128 for t in range(4)]
    starts += [high * 64, (1 - high) * 64, core * 32, (1 - core) * 32]
    at = jnp.stack(starts).astype(jnp.int32)
    stage = lax.optimization_barrier

    pair = jnp.concatenate([inputs, swap_row(inputs, 1)])
    x0 = jnp.concatenate([pair, swap_row(pair, 2)])
    by_group = stage(jnp.transpose(grad_out, (1, 0, 2)))
    groups = [
        lax.dynamic_index_in_dim(by_group, (me + s) % 4, 0, keepdims=False) for s in range(4)
    ]
    blocks = [groups[0]] + [move_x(groups[s], s) for s in (1, 2, 3)]
    near, x0 = stage((jnp.concatenate(blocks), x0))

    far = swap_z(near)
    near1, near3 = move_y(near, 1), move_y(near, -1)
    near1, near3, x0 = stage((near1, near3, x0))

    near2a, near2b = move_y(near1[0:64], 1), move_y(near3[64:128], -1)
    x1, x3 = move_x(x0, 1), move_x(x0, -1)
    near2a, near2b, far, x1, x3 = stage((near2a, near2b, far, x1, x3))

    far1, far3 = move_y(far, 1), move_y(far, -1)
    own = jnp.concatenate([near, near1, near3, near2a, near2b])
    other = swap_cores(own)
    x2a, x2b = move_x(x1[0:256], 1), move_x(x3[256:512], -1)
    far1, far3, other, x2a, x2b = stage((far1, far3, other, x2a, x2b))

    far2a, far2b = move_y(far1[0:64], 1), move_y(far3[64:128], -1)
    far_own = jnp.concatenate([far, far1, far3])
    far_other = swap_cores(far_own)
    x_near, x_far = arrange(at, (x0, x1, x2a, x2b, x3))
    gradient = near_product(x_near, own, other)
    far2a, far2b, gradient = stage((far2a, far2b, gradient))

    far_last = jnp.concatenate([far2a, far2b])
    far_other_last = swap_cores(far_last)
    gradient, column_part, row_part = far_product(
        x_far, far_own, far_last, far_other, far_other_last, gradient
    )
    column_state, sums = weigh(
        gradient, column_moment[None], over_col(column_part), row_part
    )
    row_state, totals = totals_of(row_moment[None], over_dp_row(sums))
    update, row_mean = clip(gradient, row_state, column_state, over_col(totals))
    return (update, row_state[0], column_state[0], row_mean[0, 0])


def solution(mesh):
    return jax.shard_map(
        per_device,
        mesh=mesh,
        in_specs=(
            P(("dp", "row"), "col"),
            P(("dp", "col"), None, "row"),
            P("col"),
            P(("dp", "row")),
        ),
        out_specs=(P("col", ("dp", "row")), P("col"), P(("dp", "row")), P()),
        check_vma=False,
    )
```

```python
import jax
import jax.numpy as jnp
from jax import lax
from jax.experimental import pallas as pl
from jax.experimental.pallas import tpu as pltpu
from jax.sharding import PartitionSpec as P

D = 8192
FF = 32768
VMEM_LIMIT = 18 * 1024 * 1024
COLS = 512
PLACES = (0, 1, 3, 2)
FIRST = [(s, t, far) for t in PLACES for s, far in ((0, 0), (1, 0), (2, 0), (3, 0), (0, 1))]
SECOND = [(s, t, 1) for t in PLACES for s in (1, 2, 3)]


def arrange_kernel(at_ref, x0_ref, x1_ref, x2a_ref, x2b_ref, x3_ref, first_ref, second_ref, x2_ref):
    half = x2a_ref.shape[0]
    x2_ref[0:half, :] = x2a_ref[...]
    x2_ref[half:, :] = x2b_ref[...]
    pieces = (x0_ref, x1_ref, x2_ref, x3_ref)

    for order, out_ref in ((FIRST, first_ref), (SECOND, second_ref)):
        blocks = [block + (other,) for other in (0, 1) for block in order]
        for k in range(len(blocks) // 4):
            rows = []
            for s, t, far, other in blocks[4 * k : 4 * k + 4]:
                start = pl.multiple_of(at_ref[t] + at_ref[4 + far] + at_ref[6 + other], 32)
                rows.append(pieces[s][pl.ds(start, 32), :])
            out_ref[:, k * 128 : (k + 1) * 128] = jnp.concatenate(rows, axis=0).T


def arrange(at, pieces):
    whole = pl.BlockSpec(memory_space=pltpu.VMEM)
    return pl.pallas_call(
        arrange_kernel,
        in_specs=[pl.BlockSpec(memory_space=pltpu.SMEM)] + [whole] * 5,
        out_specs=[whole] * 2,
        out_shape=[
            jax.ShapeDtypeStruct((512, 1280), jnp.bfloat16),
            jax.ShapeDtypeStruct((512, 768), jnp.bfloat16),
        ],
        scratch_shapes=[pltpu.VMEM((512, 512), jnp.bfloat16)],
        compiler_params=PARAMS,
        cost_estimate=pl.CostEstimate(flops=0, bytes_accessed=4 << 20, transcendentals=0),
    )(at, *pieces)


def first_kernel(x_ref, own_ref, other_ref, out_ref):
    out_ref[...] = jnp.dot(
        x_ref[:, 0:640], own_ref[...], preferred_element_type=jnp.float32
    ) + jnp.dot(x_ref[:, 640:1280], other_ref[...], preferred_element_type=jnp.float32)


def across(value):
    part = value[:, 0:128]
    for k in range(1, COLS // 128):
        part = part + value[:, k * 128 : (k + 1) * 128]
    return part


def gather_rows(step, part, acc_ref, row_ref):
    @pl.when(step == 0)
    def _():
        acc_ref[...] = part

    @pl.when(step > 0)
    def _():
        acc_ref[...] += part

    @pl.when(step == pl.num_programs(0) - 1)
    def _():
        row_ref[...] = jnp.sum(acc_ref[...].T, axis=0, keepdims=True)


def second_kernel(
    x_ref, own_ref, other_ref, first_ref, out_ref, col_ref, row_ref, acc_ref
):
    value = first_ref[...]
    value += jnp.dot(x_ref[:, 0:384], own_ref[...], preferred_element_type=jnp.float32)
    value += jnp.dot(x_ref[:, 384:768], other_ref[...], preferred_element_type=jnp.float32)
    out_ref[...] = value
    squares = value * value + 1e-30
    col_ref[...] = jnp.sum(squares, axis=0, keepdims=True)
    gather_rows(pl.program_id(0), across(squares), acc_ref, row_ref)


def fixed(*shape):
    return pl.BlockSpec(shape, lambda j: (0, 0))


def moving(rows):
    return pl.BlockSpec((rows, COLS), lambda j: (0, j))


G_SPEC = moving(512)
PARAMS = pltpu.CompilerParams(vmem_limit_bytes=VMEM_LIMIT)
COST = pl.CostEstimate(flops=2 * 512 * 1024 * 2048, bytes_accessed=9 << 20, transcendentals=0)


def first_product(x, own, other):
    return pl.pallas_call(
        first_kernel,
        grid=(2048 // COLS,),
        in_specs=[fixed(512, 1280), moving(640), moving(640)],
        out_specs=G_SPEC,
        out_shape=jax.ShapeDtypeStruct((512, 2048), jnp.float32),
        compiler_params=PARAMS,
        cost_estimate=COST,
    )(x, own, other)


def second_product(x, own, other, first):
    return pl.pallas_call(
        second_kernel,
        grid=(2048 // COLS,),
        in_specs=[fixed(512, 768), moving(384), moving(384), G_SPEC],
        out_specs=[G_SPEC, moving(1), fixed(1, 512)],
        out_shape=[
            jax.ShapeDtypeStruct((512, 2048), jnp.float32),
            jax.ShapeDtypeStruct((1, 2048), jnp.float32),
            jax.ShapeDtypeStruct((1, 512), jnp.float32),
        ],
        scratch_shapes=[pltpu.VMEM((512, 128), jnp.float32)],
        compiler_params=PARAMS,
        cost_estimate=COST,
    )(x, own, other, first)


def weigh_kernel(g_ref, moment_ref, sums_ref, row_ref, state_ref, out_ref, acc_ref, weighed_ref):
    step = pl.program_id(0)
    state = 0.8 * moment_ref[...] + 0.2 * sums_ref[...] / D
    state_ref[...] = state
    scaled = g_ref[...] * lax.rsqrt(state)
    gather_rows(step, across(scaled * scaled), acc_ref, weighed_ref)

    @pl.when(step == pl.num_programs(0) - 1)
    def _():
        out_ref[0:1, :] = row_ref[...]
        out_ref[1:2, :] = weighed_ref[...]


def weigh(g, column_moment, column_sums, row_part):
    return pl.pallas_call(
        weigh_kernel,
        grid=(2048 // COLS,),
        in_specs=[G_SPEC, moving(1), moving(1), fixed(1, 512)],
        out_specs=[moving(1), fixed(2, 512)],
        out_shape=[
            jax.ShapeDtypeStruct((1, 2048), jnp.float32),
            jax.ShapeDtypeStruct((2, 512), jnp.float32),
        ],
        scratch_shapes=[
            pltpu.VMEM((512, 128), jnp.float32),
            pltpu.VMEM((1, 512), jnp.float32),
        ],
        compiler_params=PARAMS,
        cost_estimate=pl.CostEstimate(
            flops=4 * 512 * 2048, bytes_accessed=4 << 20, transcendentals=0
        ),
    )(g, column_moment, column_sums, row_part)


def totals_kernel(moment_ref, sums_ref, state_ref, total_ref):
    state = 0.8 * moment_ref[...] + 0.2 * sums_ref[0:1, :] / FF
    state_ref[...] = state
    squares = jnp.sum(sums_ref[1:2, :] / state)
    lane = lax.broadcasted_iota(jnp.int32, (1, 128), 1)
    total_ref[...] = jnp.where(lane == 0, squares, jnp.where(lane == 1, jnp.sum(state), 0.0))


def totals_of(row_moment, sums):
    return pl.pallas_call(
        totals_kernel,
        out_shape=[
            jax.ShapeDtypeStruct((1, 512), jnp.float32),
            jax.ShapeDtypeStruct((1, 128), jnp.float32),
        ],
        compiler_params=PARAMS,
        cost_estimate=pl.CostEstimate(flops=2048, bytes_accessed=8192, transcendentals=0),
    )(row_moment, sums)


def clip_kernel(g_ref, row_ref, col_ref, totals_ref, out_ref, mean_ref, rows_ref):
    @pl.when(pl.program_id(0) == 0)
    def _():
        rows_ref[...] = jnp.broadcast_to(lax.rsqrt(row_ref[...]), (128, 512)).T

    lane = lax.broadcasted_iota(jnp.int32, (1, 128), 1)
    totals = totals_ref[...]
    total = jnp.sum(jnp.where(lane == 0, totals, 0.0), axis=1, keepdims=True)
    row_mean = jnp.sum(jnp.where(lane == 1, totals, 0.0), axis=1, keepdims=True) / D
    mean_ref[...] = row_mean
    clip_ratio = jnp.sqrt(row_mean * total / (D * FF))
    factor = jnp.sqrt(row_mean) / jnp.maximum(1.0, clip_ratio)
    columns = lax.rsqrt(col_ref[...]) * factor
    rows = rows_ref[...]
    for k in range(COLS // 128):
        piece = slice(k * 128, (k + 1) * 128)
        out_ref[:, piece] = g_ref[:, piece] * rows * columns[:, piece]


def clip(g, row_state, column_state, totals):
    return pl.pallas_call(
        clip_kernel,
        grid=(2048 // COLS,),
        in_specs=[G_SPEC, fixed(1, 512), moving(1), fixed(1, 128)],
        out_specs=[G_SPEC, fixed(1, 1)],
        out_shape=[
            jax.ShapeDtypeStruct((512, 2048), jnp.float32),
            jax.ShapeDtypeStruct((1, 1), jnp.float32),
        ],
        scratch_shapes=[pltpu.VMEM((512, 128), jnp.float32)],
        compiler_params=PARAMS,
        cost_estimate=pl.CostEstimate(
            flops=2 * 512 * 2048, bytes_accessed=8 << 20, transcendentals=0
        ),
    )(g, row_state, column_state, totals)


def cyclic(size, stride, shift):
    total = size * stride
    return [(j, (j + shift * stride) % total) for j in range(total)]


def flipped(total, mask):
    return [(j, j ^ mask) for j in range(total)]


def swap_cores(value):
    return lax.ppermute(value, "col", flipped(16, 1))


def move_x(value, shift):
    return lax.ppermute(value, "dp", cyclic(4, 1, shift % 4))


def move_y(value, shift):
    return lax.ppermute(value, "col", cyclic(4, 4, shift % 4))


def swap_row(value, mask):
    return lax.ppermute(value, "row", flipped(4, mask))


def swap_z(value):
    return lax.ppermute(value, "col", flipped(16, 2))


def over(value, axis, stride):
    size = 16 if axis == "col" else 4
    a, b, c = [
        lax.ppermute(value, axis, flipped(size, mask * stride)) for mask in (2, 1, 3)
    ]
    return (value + b) + (a + c)


def over_col(value):
    return over(over(value, "col", 1), "col", 4)


def over_dp_row(value):
    return over(over(value, "dp", 1), "row", 1)


def per_device(inputs, grad_out, row_moment, column_moment):
    me = lax.axis_index("dp")
    low = lax.axis_index("row")
    col = lax.axis_index("col")
    y, high, core = col // 4, col // 2 % 2, col % 2
    starts = [(low ^ ((y - t) % 4)) * 128 for t in range(4)]
    starts += [high * 64, (1 - high) * 64, core * 32, (1 - core) * 32]
    at = jnp.stack(starts).astype(jnp.int32)
    stage = lax.optimization_barrier

    pair = jnp.concatenate([inputs, swap_row(inputs, 1)])
    by_group, pair = stage((jnp.transpose(grad_out, (1, 0, 2)), pair))
    groups = [
        lax.dynamic_index_in_dim(by_group, (me + s) % 4, 0, keepdims=False) for s in range(4)
    ]
    far0 = swap_z(groups[0])
    blocks = [move_x(groups[s], s) for s in (1, 2, 3)]
    x0 = jnp.concatenate([pair, swap_row(pair, 2)])
    first = jnp.concatenate([groups[0]] + blocks + [far0])
    first, rest, x0 = stage((first, jnp.concatenate(blocks), x0))

    far = swap_z(rest)
    first1, first3 = move_y(first, 1), move_y(first, -1)
    x1, x3 = move_x(x0, 1), move_x(x0, -1)
    first1, first3, x1, x3 = stage((first1, first3, x1, x3))

    first2a, first2b = move_y(first1[0:80], 1), move_y(first3[80:160], -1)
    x2a, x2b = move_x(x1[0:256], 1), move_x(x3[256:512], -1)
    first2a, first2b, far, x2a, x2b = stage((first2a, first2b, far, x2a, x2b))

    far1, far3 = move_y(far, 1), move_y(far, -1)
    own = jnp.concatenate([first, first1, first3, first2a, first2b])
    other = swap_cores(own)
    x_first, x_second = arrange(at, (x0, x1, x2a, x2b, x3))
    far1, far3, other, x_first, x_second = stage((far1, far3, other, x_first, x_second))

    far2a, far2b = move_y(far1[0:48], 1), move_y(far3[48:96], -1)
    gradient = first_product(x_first, own, other)
    far2a, far2b, gradient = stage((far2a, far2b, gradient))

    far_own = jnp.concatenate([far, far1, far3, far2a, far2b])
    far_other = swap_cores(far_own)
    gradient, column_part, row_part = second_product(
        x_second, far_own, far_other, gradient
    )
    column_state, sums = weigh(
        gradient, column_moment[None], over_col(column_part), row_part
    )
    row_state, totals = totals_of(row_moment[None], over_dp_row(sums))
    update, row_mean = clip(gradient, row_state, column_state, over_col(totals))
    return (update, row_state[0], column_state[0], row_mean[0, 0])


def solution(mesh):
    return jax.shard_map(
        per_device,
        mesh=mesh,
        in_specs=(
            P(("dp", "row"), "col"),
            P(("dp", "col"), None, "row"),
            P("col"),
            P(("dp", "row")),
        ),
        out_specs=(P("col", ("dp", "row")), P("col"), P(("dp", "row")), P()),
        check_vma=False,
    )
```

```python
import jax
import jax.numpy as jnp
from jax import lax
from jax.experimental import pallas as pl
from jax.experimental.pallas import tpu as pltpu
from jax.sharding import PartitionSpec as P

D = 8192
FF = 32768
VMEM_LIMIT = 18 * 1024 * 1024
COLS = 512
PLACES = (0, 1, 3, 2)
FIRST = [(s, t, far) for t in PLACES for s, far in ((0, 0), (1, 0), (2, 0), (3, 0), (0, 1))]
SECOND = [(s, t, 1) for t in PLACES for s in (1, 2, 3)]


def arrange_kernel(at_ref, x0_ref, x1_ref, x2a_ref, x2b_ref, x3_ref, first_ref, second_ref, x2_ref):
    half = x2a_ref.shape[0]
    x2_ref[0:half, :] = x2a_ref[...]
    x2_ref[half:, :] = x2b_ref[...]
    pieces = (x0_ref, x1_ref, x2_ref, x3_ref)

    for order, out_ref in ((FIRST, first_ref), (SECOND, second_ref)):
        blocks = [block + (other,) for other in (0, 1) for block in order]
        for k in range(len(blocks) // 4):
            rows = []
            for s, t, far, other in blocks[4 * k : 4 * k + 4]:
                start = pl.multiple_of(at_ref[t] + at_ref[4 + far] + at_ref[6 + other], 32)
                rows.append(pieces[s][pl.ds(start, 32), :])
            out_ref[:, k * 128 : (k + 1) * 128] = jnp.concatenate(rows, axis=0).T


def arrange(at, pieces):
    whole = pl.BlockSpec(memory_space=pltpu.VMEM)
    return pl.pallas_call(
        arrange_kernel,
        in_specs=[pl.BlockSpec(memory_space=pltpu.SMEM)] + [whole] * 5,
        out_specs=[whole] * 2,
        out_shape=[
            jax.ShapeDtypeStruct((512, 1280), jnp.bfloat16),
            jax.ShapeDtypeStruct((512, 768), jnp.bfloat16),
        ],
        scratch_shapes=[pltpu.VMEM((512, 512), jnp.bfloat16)],
        compiler_params=PARAMS,
        cost_estimate=pl.CostEstimate(flops=0, bytes_accessed=4 << 20, transcendentals=0),
    )(at, *pieces)


def first_kernel(x_ref, own_ref, other_ref, out_ref):
    out_ref[...] = jnp.dot(
        x_ref[:, 0:640], own_ref[...], preferred_element_type=jnp.float32
    ) + jnp.dot(x_ref[:, 640:1280], other_ref[...], preferred_element_type=jnp.float32)


def across(value):
    part = value[:, 0:128]
    for k in range(1, COLS // 128):
        part = part + value[:, k * 128 : (k + 1) * 128]
    return part


def gather_rows(step, part, acc_ref, row_ref):
    @pl.when(step == 0)
    def _():
        acc_ref[...] = part

    @pl.when(step > 0)
    def _():
        acc_ref[...] += part

    @pl.when(step == pl.num_programs(0) - 1)
    def _():
        row_ref[...] = jnp.sum(acc_ref[...].T, axis=0, keepdims=True)


def second_kernel(
    x_ref, own_ref, other_ref, first_ref, out_ref, col_ref, row_ref, acc_ref
):
    value = first_ref[...]
    value += jnp.dot(x_ref[:, 0:384], own_ref[...], preferred_element_type=jnp.float32)
    value += jnp.dot(x_ref[:, 384:768], other_ref[...], preferred_element_type=jnp.float32)
    out_ref[...] = value
    squares = value * value + 1e-30
    col_ref[...] = jnp.sum(squares, axis=0, keepdims=True)
    gather_rows(pl.program_id(0), across(squares), acc_ref, row_ref)


def fixed(*shape):
    return pl.BlockSpec(shape, lambda j: (0, 0))


def moving(rows):
    return pl.BlockSpec((rows, COLS), lambda j: (0, j))


def in_hbm(value):
    return pltpu.with_memory_space_constraint(value, pltpu.HBM)


G_SPEC = moving(512)
PARAMS = pltpu.CompilerParams(vmem_limit_bytes=VMEM_LIMIT)
COST = pl.CostEstimate(flops=2 * 512 * 1024 * 2048, bytes_accessed=9 << 20, transcendentals=0)


def first_product(x, own, other):
    return pl.pallas_call(
        first_kernel,
        grid=(2048 // COLS,),
        in_specs=[fixed(512, 1280), moving(640), moving(640)],
        out_specs=G_SPEC,
        out_shape=jax.ShapeDtypeStruct((512, 2048), jnp.float32),
        compiler_params=PARAMS,
        cost_estimate=COST,
    )(x, own, other)


def second_product(x, own, other, first):
    return pl.pallas_call(
        second_kernel,
        grid=(2048 // COLS,),
        in_specs=[fixed(512, 768), moving(384), moving(384), G_SPEC],
        out_specs=[G_SPEC, moving(1), fixed(1, 512)],
        out_shape=[
            pltpu.HBM((512, 2048), jnp.float32),
            jax.ShapeDtypeStruct((1, 2048), jnp.float32),
            jax.ShapeDtypeStruct((1, 512), jnp.float32),
        ],
        scratch_shapes=[pltpu.VMEM((512, 128), jnp.float32)],
        compiler_params=PARAMS,
        cost_estimate=COST,
    )(x, own, other, first)


def weigh_kernel(g_ref, moment_ref, parts_ref, row_ref, state_ref, out_ref, acc_ref, weighed_ref):
    step = pl.program_id(0)
    sums = jnp.sum(parts_ref[...], axis=0, keepdims=True)
    state = 0.8 * moment_ref[...] + 0.2 * sums / D
    state_ref[...] = state
    scaled = g_ref[...] * lax.rsqrt(state)
    gather_rows(step, across(scaled * scaled), acc_ref, weighed_ref)

    @pl.when(step == pl.num_programs(0) - 1)
    def _():
        out_ref[:, 0:512] = row_ref[...]
        out_ref[:, 512:1024] = weighed_ref[...]


def weigh(g, column_moment, column_parts, row_part):
    return pl.pallas_call(
        weigh_kernel,
        grid=(2048 // COLS,),
        in_specs=[G_SPEC, moving(1), moving(16), fixed(1, 512)],
        out_specs=[moving(1), fixed(1, 1024)],
        out_shape=[
            jax.ShapeDtypeStruct((1, 2048), jnp.float32),
            jax.ShapeDtypeStruct((1, 1024), jnp.float32),
        ],
        scratch_shapes=[
            pltpu.VMEM((512, 128), jnp.float32),
            pltpu.VMEM((1, 512), jnp.float32),
        ],
        compiler_params=PARAMS,
        cost_estimate=pl.CostEstimate(
            flops=4 * 512 * 2048, bytes_accessed=4 << 20, transcendentals=0
        ),
    )(in_hbm(g), column_moment, column_parts, row_part)


def totals_kernel(moment_ref, parts_ref, state_ref, total_ref):
    sums = jnp.sum(parts_ref[...], axis=0, keepdims=True)
    state = 0.8 * moment_ref[...] + 0.2 * sums[:, 0:512] / FF
    state_ref[...] = state
    squares = jnp.sum(sums[:, 512:1024] / state)
    lane = lax.broadcasted_iota(jnp.int32, (1, 128), 1)
    total_ref[...] = jnp.where(lane == 0, squares, jnp.where(lane == 1, jnp.sum(state), 0.0))


def totals_of(row_moment, parts):
    return pl.pallas_call(
        totals_kernel,
        out_shape=[
            jax.ShapeDtypeStruct((1, 512), jnp.float32),
            jax.ShapeDtypeStruct((1, 128), jnp.float32),
        ],
        compiler_params=PARAMS,
        cost_estimate=pl.CostEstimate(flops=16384, bytes_accessed=70000, transcendentals=0),
    )(row_moment, parts)


def clip_kernel(g_ref, row_ref, col_ref, totals_ref, out_ref, mean_ref, rows_ref):
    @pl.when(pl.program_id(0) == 0)
    def _():
        rows_ref[...] = jnp.broadcast_to(lax.rsqrt(row_ref[...]), (128, 512)).T

    lane = lax.broadcasted_iota(jnp.int32, (1, 128), 1)
    totals = jnp.sum(totals_ref[...], axis=0, keepdims=True)
    total = jnp.sum(jnp.where(lane == 0, totals, 0.0), axis=1, keepdims=True)
    row_mean = jnp.sum(jnp.where(lane == 1, totals, 0.0), axis=1, keepdims=True) / D
    mean_ref[...] = row_mean
    clip_ratio = jnp.sqrt(row_mean * total / (D * FF))
    factor = jnp.sqrt(row_mean) / jnp.maximum(1.0, clip_ratio)
    columns = lax.rsqrt(col_ref[...]) * factor
    rows = rows_ref[...]
    for k in range(COLS // 128):
        piece = slice(k * 128, (k + 1) * 128)
        out_ref[:, piece] = g_ref[:, piece] * rows * columns[:, piece]


def clip(g, row_state, column_state, totals):
    return pl.pallas_call(
        clip_kernel,
        grid=(2048 // COLS,),
        in_specs=[G_SPEC, fixed(1, 512), moving(1), fixed(16, 128)],
        out_specs=[G_SPEC, fixed(1, 1)],
        out_shape=[
            jax.ShapeDtypeStruct((512, 2048), jnp.float32),
            jax.ShapeDtypeStruct((1, 1), jnp.float32),
        ],
        scratch_shapes=[pltpu.VMEM((512, 128), jnp.float32)],
        compiler_params=PARAMS,
        cost_estimate=pl.CostEstimate(
            flops=2 * 512 * 2048, bytes_accessed=8 << 20, transcendentals=0
        ),
    )(in_hbm(g), row_state, column_state, totals)


def cyclic(size, stride, shift):
    total = size * stride
    return [(j, (j + shift * stride) % total) for j in range(total)]


def flipped(total, mask):
    return [(j, j ^ mask) for j in range(total)]


def swap_cores(value):
    return lax.ppermute(value, "col", flipped(16, 1))


def move_x(value, shift):
    return lax.ppermute(value, "dp", cyclic(4, 1, shift % 4))


def move_y(value, shift):
    return lax.ppermute(value, "col", cyclic(4, 4, shift % 4))


def swap_row(value, mask):
    return lax.ppermute(value, "row", flipped(4, mask))


def swap_z(value):
    return lax.ppermute(value, "col", flipped(16, 2))


def copies(value, axis):
    rows = jnp.broadcast_to(value, (16,) + value.shape)
    return lax.all_to_all(rows, axis, 0, 0).reshape(16, value.shape[1])


def per_device(inputs, grad_out, row_moment, column_moment):
    me = lax.axis_index("dp")
    low = lax.axis_index("row")
    col = lax.axis_index("col")
    y, high, core = col // 4, col // 2 % 2, col % 2
    starts = [(low ^ ((y - t) % 4)) * 128 for t in range(4)]
    starts += [high * 64, (1 - high) * 64, core * 32, (1 - core) * 32]
    at = jnp.stack(starts).astype(jnp.int32)
    stage = lax.optimization_barrier

    pair = jnp.concatenate([inputs, swap_row(inputs, 1)])
    by_group = stage(jnp.transpose(grad_out, (1, 0, 2)))
    groups = [
        lax.dynamic_index_in_dim(by_group, (me + s) % 4, 0, keepdims=False) for s in range(4)
    ]
    far0 = swap_z(groups[0])
    blocks = [move_x(groups[s], s) for s in (1, 2, 3)]
    first = jnp.concatenate([groups[0]] + blocks + [far0])
    first, rest, pair = stage((first, jnp.concatenate(blocks), pair))

    far = swap_z(rest)
    first1, first3 = move_y(first, 1), move_y(first, -1)
    x0 = jnp.concatenate([pair, swap_row(pair, 2)])
    first1, first3, x0 = stage((first1, first3, x0))

    first2a, first2b = move_y(first1[0:80], 1), move_y(first3[80:160], -1)
    x1, x3 = move_x(x0, 1), move_x(x0, -1)
    first2a, first2b, far, x1, x3 = stage((first2a, first2b, far, x1, x3))

    far1, far3 = move_y(far, 1), move_y(far, -1)
    own = jnp.concatenate([first, first1, first3, first2a, first2b])
    other = swap_cores(own)
    x2a, x2b = move_x(x1[0:256], 1), move_x(x3[256:512], -1)
    far1, far3, other, x2a, x2b = stage((far1, far3, other, x2a, x2b))

    far2a, far2b = move_y(far1[0:48], 1), move_y(far3[48:96], -1)
    x_first, x_second = arrange(at, (x0, x1, x2a, x2b, x3))
    gradient = first_product(x_first, own, other)
    far2a, far2b, gradient = stage((far2a, far2b, gradient))

    far_own = jnp.concatenate([far, far1, far3, far2a, far2b])
    far_other = swap_cores(far_own)
    gradient, column_part, row_part = second_product(
        x_second, far_own, far_other, gradient
    )
    column_state, sums = weigh(
        gradient, column_moment[None], copies(column_part, "col"), row_part
    )
    row_state, totals = totals_of(row_moment[None], copies(sums, ("dp", "row")))
    update, row_mean = clip(gradient, row_state, column_state, copies(totals, "col"))
    return (update, row_state[0], column_state[0], row_mean[0, 0])


def solution(mesh):
    return jax.shard_map(
        per_device,
        mesh=mesh,
        in_specs=(
            P(("dp", "row"), "col"),
            P(("dp", "col"), None, "row"),
            P("col"),
            P(("dp", "row")),
        ),
        out_specs=(P("col", ("dp", "row")), P("col"), P(("dp", "row")), P()),
        check_vma=False,
    )
```

```python
import jax
import jax.numpy as jnp
from jax import lax
from jax.experimental import pallas as pl
from jax.experimental.pallas import tpu as pltpu
from jax.sharding import PartitionSpec as P

D = 8192
FF = 32768
VMEM_LIMIT = 18 * 1024 * 1024
COLS = 512
FIRST = ((0, 0), (1, 0), (2, 0), (3, 0), (0, 1))
FAR = ((1, 1), (2, 1), (3, 1))
PARTS = (
    [(s, t, far) for t in (0, 1, 3) for s, far in FIRST],
    [(s, 2, far) for s, far in FIRST] + [(s, t, far) for t in (0, 1, 3) for s, far in FAR],
    [(s, 2, far) for s, far in FAR],
)


def arrange_kernel(at_ref, x0_ref, x1_ref, x2a_ref, x2b_ref, x3_ref, a_ref, b_ref, c_ref, x2_ref):
    half = x2a_ref.shape[0]
    x2_ref[0:half, :] = x2a_ref[...]
    x2_ref[half:, :] = x2b_ref[...]
    pieces = (x0_ref, x1_ref, x2_ref, x3_ref)

    for part, out_ref in zip(PARTS, (a_ref, b_ref, c_ref)):
        blocks = [block + (other,) for other in (0, 1) for block in part]
        for k in range(0, len(blocks), 4):
            rows = []
            for s, t, far, other in blocks[k : k + 4]:
                start = pl.multiple_of(at_ref[t] + at_ref[4 + far] + at_ref[6 + other], 32)
                rows.append(pieces[s][pl.ds(start, 32), :])
            out_ref[:, k * 32 : (k + len(rows)) * 32] = jnp.concatenate(rows, axis=0).T


def arrange(at, pieces):
    whole = pl.BlockSpec(memory_space=pltpu.VMEM)
    return pl.pallas_call(
        arrange_kernel,
        in_specs=[pl.BlockSpec(memory_space=pltpu.SMEM)] + [whole] * 5,
        out_specs=[whole] * 3,
        out_shape=[
            jax.ShapeDtypeStruct((512, 64 * len(part)), jnp.bfloat16) for part in PARTS
        ],
        scratch_shapes=[pltpu.VMEM((512, 512), jnp.bfloat16)],
        compiler_params=PARAMS,
        cost_estimate=pl.CostEstimate(flops=0, bytes_accessed=4 << 20, transcendentals=0),
    )(at, *pieces)


def both(x_ref, own_ref, other_ref):
    rows = own_ref.shape[0]
    return jnp.dot(
        x_ref[:, 0:rows], own_ref[...], preferred_element_type=jnp.float32
    ) + jnp.dot(x_ref[:, rows : 2 * rows], other_ref[...], preferred_element_type=jnp.float32)


def start_kernel(x_ref, own_ref, other_ref, out_ref):
    out_ref[...] = both(x_ref, own_ref, other_ref)


def add_kernel(x_ref, own_ref, other_ref, before_ref, out_ref):
    out_ref[...] = before_ref[...] + both(x_ref, own_ref, other_ref)


def across(value):
    part = value[:, 0:128]
    for k in range(1, COLS // 128):
        part = part + value[:, k * 128 : (k + 1) * 128]
    return part


def gather_rows(step, part, acc_ref, row_ref):
    @pl.when(step == 0)
    def _():
        acc_ref[...] = part

    @pl.when(step > 0)
    def _():
        acc_ref[...] += part

    @pl.when(step == pl.num_programs(0) - 1)
    def _():
        row_ref[...] = jnp.sum(acc_ref[...].T, axis=0, keepdims=True)


def last_kernel(x_ref, own_ref, other_ref, before_ref, out_ref, col_ref, row_ref, acc_ref):
    value = before_ref[...] + both(x_ref, own_ref, other_ref)
    out_ref[...] = value
    squares = value * value + 1e-30
    col_ref[...] = jnp.sum(squares, axis=0, keepdims=True)
    gather_rows(pl.program_id(0), across(squares), acc_ref, row_ref)


def fixed(*shape):
    return pl.BlockSpec(shape, lambda j: (0, 0))


def moving(rows):
    return pl.BlockSpec((rows, COLS), lambda j: (0, j))


def in_vmem(value):
    return pltpu.with_memory_space_constraint(value, pltpu.VMEM)


G_SPEC = moving(512)
PARAMS = pltpu.CompilerParams(vmem_limit_bytes=VMEM_LIMIT)


def cost_of(x):
    return pl.CostEstimate(
        flops=2 * 512 * x.shape[1] * 2048, bytes_accessed=9 << 20, transcendentals=0
    )


def product(x, own, other, before=None):
    rows = own.shape[0]
    specs = [fixed(512, 2 * rows), moving(rows), moving(rows)]
    operands = [x, own, other]
    if before is not None:
        specs.append(G_SPEC)
        operands.append(before)
    return pl.pallas_call(
        start_kernel if before is None else add_kernel,
        grid=(2048 // COLS,),
        in_specs=specs,
        out_specs=G_SPEC,
        out_shape=jax.ShapeDtypeStruct((512, 2048), jnp.float32),
        compiler_params=PARAMS,
        cost_estimate=cost_of(x),
    )(*operands)


def last_product(x, own, other, before):
    rows = own.shape[0]
    return pl.pallas_call(
        last_kernel,
        grid=(2048 // COLS,),
        in_specs=[fixed(512, 2 * rows), moving(rows), moving(rows), G_SPEC],
        out_specs=[G_SPEC, moving(1), fixed(1, 512)],
        out_shape=[
            pltpu.VMEM((512, 2048), jnp.float32),
            jax.ShapeDtypeStruct((1, 2048), jnp.float32),
            jax.ShapeDtypeStruct((1, 512), jnp.float32),
        ],
        scratch_shapes=[pltpu.VMEM((512, 128), jnp.float32)],
        compiler_params=PARAMS,
        cost_estimate=cost_of(x),
    )(x, own, other, before)


def weigh_kernel(g_ref, moment_ref, parts_ref, row_ref, state_ref, out_ref, acc_ref, weighed_ref):
    step = pl.program_id(0)
    sums = jnp.sum(parts_ref[...], axis=0, keepdims=True)
    state = 0.8 * moment_ref[...] + 0.2 * sums / D
    state_ref[...] = state
    scaled = g_ref[...] * lax.rsqrt(state)
    gather_rows(step, across(scaled * scaled), acc_ref, weighed_ref)

    @pl.when(step == pl.num_programs(0) - 1)
    def _():
        out_ref[:, 0:512] = row_ref[...]
        out_ref[:, 512:1024] = weighed_ref[...]


def weigh(g, column_moment, column_parts, row_part):
    return pl.pallas_call(
        weigh_kernel,
        grid=(2048 // COLS,),
        in_specs=[G_SPEC, moving(1), moving(16), fixed(1, 512)],
        out_specs=[moving(1), fixed(1, 1024)],
        out_shape=[
            jax.ShapeDtypeStruct((1, 2048), jnp.float32),
            jax.ShapeDtypeStruct((1, 1024), jnp.float32),
        ],
        scratch_shapes=[
            pltpu.VMEM((512, 128), jnp.float32),
            pltpu.VMEM((1, 512), jnp.float32),
        ],
        compiler_params=PARAMS,
        cost_estimate=pl.CostEstimate(
            flops=4 * 512 * 2048, bytes_accessed=4 << 20, transcendentals=0
        ),
    )(in_vmem(g), column_moment, column_parts, row_part)


def totals_kernel(moment_ref, parts_ref, state_ref, total_ref):
    sums = jnp.sum(parts_ref[...], axis=0, keepdims=True)
    state = 0.8 * moment_ref[...] + 0.2 * sums[:, 0:512] / FF
    state_ref[...] = state
    squares = jnp.sum(sums[:, 512:1024] / state)
    lane = lax.broadcasted_iota(jnp.int32, (1, 128), 1)
    total_ref[...] = jnp.where(lane == 0, squares, jnp.where(lane == 1, jnp.sum(state), 0.0))


def totals_of(row_moment, parts):
    return pl.pallas_call(
        totals_kernel,
        out_shape=[
            jax.ShapeDtypeStruct((1, 512), jnp.float32),
            jax.ShapeDtypeStruct((1, 128), jnp.float32),
        ],
        compiler_params=PARAMS,
        cost_estimate=pl.CostEstimate(flops=16384, bytes_accessed=70000, transcendentals=0),
    )(row_moment, parts)


def clip_kernel(g_ref, row_ref, col_ref, totals_ref, out_ref, mean_ref, rows_ref):
    @pl.when(pl.program_id(0) == 0)
    def _():
        rows_ref[...] = jnp.broadcast_to(lax.rsqrt(row_ref[...]), (128, 512)).T

    lane = lax.broadcasted_iota(jnp.int32, (1, 128), 1)
    totals = jnp.sum(totals_ref[...], axis=0, keepdims=True)
    total = jnp.sum(jnp.where(lane == 0, totals, 0.0), axis=1, keepdims=True)
    row_mean = jnp.sum(jnp.where(lane == 1, totals, 0.0), axis=1, keepdims=True) / D
    mean_ref[...] = row_mean
    clip_ratio = jnp.sqrt(row_mean * total / (D * FF))
    factor = jnp.sqrt(row_mean) / jnp.maximum(1.0, clip_ratio)
    columns = lax.rsqrt(col_ref[...]) * factor
    rows = rows_ref[...]
    for k in range(COLS // 128):
        piece = slice(k * 128, (k + 1) * 128)
        out_ref[:, piece] = g_ref[:, piece] * rows * columns[:, piece]


def clip(g, row_state, column_state, totals):
    return pl.pallas_call(
        clip_kernel,
        grid=(2048 // COLS,),
        in_specs=[G_SPEC, fixed(1, 512), moving(1), fixed(16, 128)],
        out_specs=[G_SPEC, fixed(1, 1)],
        out_shape=[
            jax.ShapeDtypeStruct((512, 2048), jnp.float32),
            jax.ShapeDtypeStruct((1, 1), jnp.float32),
        ],
        scratch_shapes=[pltpu.VMEM((512, 128), jnp.float32)],
        compiler_params=PARAMS,
        cost_estimate=pl.CostEstimate(
            flops=2 * 512 * 2048, bytes_accessed=8 << 20, transcendentals=0
        ),
    )(in_vmem(g), row_state, column_state, totals)


def cyclic(size, stride, shift):
    total = size * stride
    return [(j, (j + shift * stride) % total) for j in range(total)]


def flipped(total, mask):
    return [(j, j ^ mask) for j in range(total)]


def swap_cores(value):
    return lax.ppermute(value, "col", flipped(16, 1))


def move_x(value, shift):
    return lax.ppermute(value, "dp", cyclic(4, 1, shift % 4))


def move_y(value, shift):
    return lax.ppermute(value, "col", cyclic(4, 4, shift % 4))


def swap_row(value, mask):
    return lax.ppermute(value, "row", flipped(4, mask))


def swap_z(value):
    return lax.ppermute(value, "col", flipped(16, 2))


def copies(value, axis):
    rows = jnp.broadcast_to(value, (16,) + value.shape)
    return lax.all_to_all(rows, axis, 0, 0).reshape(16, value.shape[1])


def per_device(inputs, grad_out, row_moment, column_moment):
    me = lax.axis_index("dp")
    low = lax.axis_index("row")
    col = lax.axis_index("col")
    y, high, core = col // 4, col // 2 % 2, col % 2
    places = [low ^ ((y - t) % 4) for t in range(4)]
    starts = [(place % 2 * 2 + place // 2) * 128 for place in places]
    starts += [high * 64, (1 - high) * 64, core * 32, (1 - core) * 32]
    at = jnp.stack(starts).astype(jnp.int32)
    stage = lax.optimization_barrier

    pair = jnp.concatenate([inputs, swap_row(inputs, 2)])
    by_group = stage(jnp.transpose(grad_out, (1, 0, 2)))
    groups = [
        lax.dynamic_index_in_dim(by_group, (me + s) % 4, 0, keepdims=False) for s in range(4)
    ]
    far0 = swap_z(groups[0])
    blocks = [move_x(groups[s], s) for s in (1, 2, 3)]
    x0 = jnp.concatenate([pair, swap_row(pair, 1)])
    first = jnp.concatenate([groups[0]] + blocks + [far0])
    first, rest, x0 = stage((first, jnp.concatenate(blocks), x0))

    far = swap_z(rest)
    first1, first3 = move_y(first, 1), move_y(first, -1)
    x1, x3 = move_x(x0, 1), move_x(x0, -1)
    far, first1, first3, x1, x3 = stage((far, first1, first3, x1, x3))

    far1, far3 = move_y(far, 1), move_y(far, -1)
    first2a, first2b = move_y(first1[0:80], 1), move_y(first3[80:160], -1)
    own_a = jnp.concatenate([first, first1, first3])
    other_a = swap_cores(own_a)
    x2a, x2b = move_x(x1[0:256], 1), move_x(x3[256:512], -1)
    far1, far3, first2a, first2b, other_a, x2a, x2b = stage(
        (far1, far3, first2a, first2b, other_a, x2a, x2b)
    )

    far2a, far2b = move_y(far1[0:48], 1), move_y(far3[48:96], -1)
    own_b = jnp.concatenate([first2a, first2b, far, far1, far3])
    other_b = swap_cores(own_b)
    x_a, x_b, x_c = arrange(at, (x0, x1, x2a, x2b, x3))
    gradient = product(x_a, own_a, other_a)
    far2a, far2b, other_b, gradient = stage((far2a, far2b, other_b, gradient))

    own_c = jnp.concatenate([far2a, far2b])
    other_c = swap_cores(own_c)
    gradient = product(x_b, own_b, other_b, gradient)
    gradient, column_part, row_part = last_product(x_c, own_c, other_c, gradient)
    column_state, sums = weigh(
        gradient, column_moment[None], copies(column_part, "col"), row_part
    )
    row_state, totals = totals_of(row_moment[None], copies(sums, ("dp", "row")))
    update, row_mean = clip(gradient, row_state, column_state, copies(totals, "col"))
    return (update, row_state[0], column_state[0], row_mean[0, 0])


def solution(mesh):
    return jax.shard_map(
        per_device,
        mesh=mesh,
        in_specs=(
            P(("dp", "row"), "col"),
            P(("dp", "col"), None, "row"),
            P("col"),
            P(("dp", "row")),
        ),
        out_specs=(P("col", ("dp", "row")), P("col"), P(("dp", "row")), P()),
        check_vma=False,
    )
```

```python
import jax
import jax.numpy as jnp
from jax import lax
from jax.experimental import pallas as pl
from jax.experimental.pallas import tpu as pltpu
from jax.sharding import PartitionSpec as P

D = 8192
FF = 32768
VMEM_LIMIT = 20 * 1024 * 1024
COLS = 512
REPLICAS = (0, 1, 2, 3)


def arrange_kernel(at_ref, even_ref, odd_ref, near_ref, far_ref):
    for far, out_ref in ((0, near_ref), (1, far_ref)):
        for other in (0, 1):
            for t in range(4):
                start = at_ref[t] + at_ref[4 + far] + at_ref[6 + other]
                rows = []
                for s in REPLICAS:
                    piece = odd_ref if s % 2 else even_ref
                    place = pl.multiple_of(start + s // 2 * 512, 32)
                    rows.append(piece[pl.ds(place, 32), :])
                column = other * 512 + t * 128
                out_ref[:, column : column + 128] = jnp.concatenate(rows, axis=0).T


def arrange(at, even, odd):
    whole = pl.BlockSpec(memory_space=pltpu.VMEM)
    return pl.pallas_call(
        arrange_kernel,
        in_specs=[pl.BlockSpec(memory_space=pltpu.SMEM), whole, whole],
        out_specs=[whole] * 2,
        out_shape=[jax.ShapeDtypeStruct((512, 1024), jnp.bfloat16)] * 2,
        compiler_params=PARAMS,
        cost_estimate=pl.CostEstimate(flops=0, bytes_accessed=4 << 20, transcendentals=0),
    )(at, even, odd)


def near_kernel(x_ref, own_ref, other_ref, out_ref):
    out_ref[...] = jnp.dot(
        x_ref[:, 0:512], own_ref[...], preferred_element_type=jnp.float32
    ) + jnp.dot(x_ref[:, 512:1024], other_ref[...], preferred_element_type=jnp.float32)


def across(value):
    part = value[:, 0:128]
    for k in range(1, COLS // 128):
        part = part + value[:, k * 128 : (k + 1) * 128]
    return part


def gather_rows(step, part, acc_ref, row_ref):
    @pl.when(step == 0)
    def _():
        acc_ref[...] = part

    @pl.when(step > 0)
    def _():
        acc_ref[...] += part

    @pl.when(step == pl.num_programs(0) - 1)
    def _():
        row_ref[...] = jnp.sum(acc_ref[...].T, axis=0, keepdims=True)


def far_kernel(x_ref, *refs):
    blocks, (near_ref, out_ref, col_ref, row_ref, acc_ref) = refs[:8], refs[8:]
    value = near_ref[...]
    for half in (0, 1):
        g = jnp.concatenate([ref[...] for ref in blocks[4 * half : 4 * half + 4]], axis=0)
        x = x_ref[:, 512 * half : 512 * half + 512]
        value += jnp.dot(x, g, preferred_element_type=jnp.float32)
    out_ref[...] = value
    squares = value * value + 1e-30
    col_ref[...] = jnp.sum(squares, axis=0, keepdims=True)
    gather_rows(pl.program_id(0), across(squares), acc_ref, row_ref)


def fixed(*shape):
    return pl.BlockSpec(shape, lambda j: (0, 0))


def moving(rows):
    return pl.BlockSpec((rows, COLS), lambda j: (0, j))


def in_vmem(value):
    return pltpu.with_memory_space_constraint(value, pltpu.VMEM)


G_SPEC = moving(512)
PARAMS = pltpu.CompilerParams(vmem_limit_bytes=VMEM_LIMIT)


COST = pl.CostEstimate(flops=2 * 512 * 1024 * 2048, bytes_accessed=9 << 20, transcendentals=0)


def near_product(x, own, other):
    return pl.pallas_call(
        near_kernel,
        grid=(2048 // COLS,),
        in_specs=[fixed(512, 1024), moving(512), moving(512)],
        out_specs=G_SPEC,
        out_shape=jax.ShapeDtypeStruct((512, 2048), jnp.float32),
        compiler_params=PARAMS,
        cost_estimate=COST,
    )(x, own, other)


def far_product(x, blocks, near):
    return pl.pallas_call(
        far_kernel,
        grid=(2048 // COLS,),
        in_specs=[fixed(512, 1024)] + [moving(128)] * 8 + [G_SPEC],
        out_specs=[G_SPEC, moving(1), fixed(1, 512)],
        out_shape=[
            pltpu.VMEM((512, 2048), jnp.float32),
            jax.ShapeDtypeStruct((1, 2048), jnp.float32),
            jax.ShapeDtypeStruct((1, 512), jnp.float32),
        ],
        scratch_shapes=[pltpu.VMEM((512, 128), jnp.float32)],
        compiler_params=PARAMS,
        cost_estimate=COST,
    )(x, *blocks, near)


def weigh_kernel(g_ref, moment_ref, parts_ref, row_ref, state_ref, out_ref, acc_ref, weighed_ref):
    step = pl.program_id(0)
    sums = jnp.sum(parts_ref[...], axis=0, keepdims=True)
    state = 0.8 * moment_ref[...] + 0.2 * sums / D
    state_ref[...] = state
    scaled = g_ref[...] * lax.rsqrt(state)
    gather_rows(step, across(scaled * scaled), acc_ref, weighed_ref)

    @pl.when(step == pl.num_programs(0) - 1)
    def _():
        out_ref[:, 0:512] = row_ref[...]
        out_ref[:, 512:1024] = weighed_ref[...]


def weigh(g, column_moment, column_parts, row_part):
    return pl.pallas_call(
        weigh_kernel,
        grid=(2048 // COLS,),
        in_specs=[G_SPEC, moving(1), moving(16), fixed(1, 512)],
        out_specs=[moving(1), fixed(1, 1024)],
        out_shape=[
            jax.ShapeDtypeStruct((1, 2048), jnp.float32),
            jax.ShapeDtypeStruct((1, 1024), jnp.float32),
        ],
        scratch_shapes=[
            pltpu.VMEM((512, 128), jnp.float32),
            pltpu.VMEM((1, 512), jnp.float32),
        ],
        compiler_params=PARAMS,
        cost_estimate=pl.CostEstimate(
            flops=4 * 512 * 2048, bytes_accessed=4 << 20, transcendentals=0
        ),
    )(in_vmem(g), column_moment, column_parts, row_part)


def totals_kernel(moment_ref, parts_ref, state_ref, total_ref):
    sums = jnp.sum(parts_ref[...], axis=0, keepdims=True)
    state = 0.8 * moment_ref[...] + 0.2 * sums[:, 0:512] / FF
    state_ref[...] = state
    squares = jnp.sum(sums[:, 512:1024] / state)
    lane = lax.broadcasted_iota(jnp.int32, (1, 128), 1)
    total_ref[...] = jnp.where(lane == 0, squares, jnp.where(lane == 1, jnp.sum(state), 0.0))


def totals_of(row_moment, parts):
    return pl.pallas_call(
        totals_kernel,
        out_shape=[
            jax.ShapeDtypeStruct((1, 512), jnp.float32),
            jax.ShapeDtypeStruct((1, 128), jnp.float32),
        ],
        compiler_params=PARAMS,
        cost_estimate=pl.CostEstimate(flops=16384, bytes_accessed=70000, transcendentals=0),
    )(row_moment, parts)


def clip_kernel(g_ref, row_ref, col_ref, totals_ref, out_ref, mean_ref, rows_ref):
    @pl.when(pl.program_id(0) == 0)
    def _():
        rows_ref[...] = jnp.broadcast_to(lax.rsqrt(row_ref[...]), (128, 512)).T

    lane = lax.broadcasted_iota(jnp.int32, (1, 128), 1)
    totals = jnp.sum(totals_ref[...], axis=0, keepdims=True)
    total = jnp.sum(jnp.where(lane == 0, totals, 0.0), axis=1, keepdims=True)
    row_mean = jnp.sum(jnp.where(lane == 1, totals, 0.0), axis=1, keepdims=True) / D
    mean_ref[...] = row_mean
    clip_ratio = jnp.sqrt(row_mean * total / (D * FF))
    factor = jnp.sqrt(row_mean) / jnp.maximum(1.0, clip_ratio)
    columns = lax.rsqrt(col_ref[...]) * factor
    rows = rows_ref[...]
    for k in range(COLS // 128):
        piece = slice(k * 128, (k + 1) * 128)
        out_ref[:, piece] = g_ref[:, piece] * rows * columns[:, piece]


def clip(g, row_state, column_state, totals):
    return pl.pallas_call(
        clip_kernel,
        grid=(2048 // COLS,),
        in_specs=[G_SPEC, fixed(1, 512), moving(1), fixed(16, 128)],
        out_specs=[G_SPEC, fixed(1, 1)],
        out_shape=[
            jax.ShapeDtypeStruct((512, 2048), jnp.float32),
            jax.ShapeDtypeStruct((1, 1), jnp.float32),
        ],
        scratch_shapes=[pltpu.VMEM((512, 128), jnp.float32)],
        compiler_params=PARAMS,
        cost_estimate=pl.CostEstimate(
            flops=2 * 512 * 2048, bytes_accessed=8 << 20, transcendentals=0
        ),
    )(in_vmem(g), row_state, column_state, totals)


def cyclic(size, stride, shift):
    total = size * stride
    return [(j, (j + shift * stride) % total) for j in range(total)]


def flipped(total, mask):
    return [(j, j ^ mask) for j in range(total)]


def swap_cores(value):
    return lax.ppermute(value, "col", flipped(16, 1))


def swap_x(value, mask):
    return lax.ppermute(value, "dp", flipped(4, mask))


def move_y(value, shift):
    return lax.ppermute(value, "col", cyclic(4, 4, shift % 4))


def swap_row(value, mask):
    return lax.ppermute(value, "row", flipped(4, mask))


def swap_z(value):
    return lax.ppermute(value, "col", flipped(16, 2))


def copies(value, axis):
    rows = jnp.broadcast_to(value, (16,) + value.shape)
    return lax.all_to_all(rows, axis, 0, 0).reshape(16, value.shape[1])


def per_device(inputs, grad_out, row_moment, column_moment):
    me = lax.axis_index("dp")
    low = lax.axis_index("row")
    col = lax.axis_index("col")
    y, high, core = col // 4, col // 2 % 2, col % 2
    places = [low ^ ((y - t) % 4) for t in range(4)]
    starts = [(place % 2 * 2 + place // 2) * 128 for place in places]
    starts += [high * 64, (1 - high) * 64, core * 32, (1 - core) * 32]
    at = jnp.stack(starts).astype(jnp.int32)
    stage = lax.optimization_barrier

    pair = jnp.concatenate([inputs, swap_row(inputs, 2)])
    by_group = stage(jnp.transpose(grad_out, (1, 0, 2)))
    groups = [
        lax.dynamic_index_in_dim(by_group, me ^ s, 0, keepdims=False) for s in REPLICAS
    ]
    blocks = [groups[0]] + [swap_x(groups[s], s) for s in (1, 2, 3)]
    x0 = jnp.concatenate([pair, swap_row(pair, 1)])
    near, x0 = stage((jnp.concatenate(blocks), x0))

    even = jnp.concatenate([x0, swap_x(x0, 2)])
    far = swap_z(near)
    nears = [move_y(near, t) for t in (1, 2, 3)]
    far, even, *nears = stage((far, even, *nears))

    own = jnp.concatenate([near, *nears])
    other = swap_cores(own)
    odd = swap_x(even, 1)
    fars = [move_y(far, t) for t in (1, 2, 3)]
    other, odd, *fars = stage((other, odd, *fars))

    fars = [far, *fars]
    others = [swap_cores(block) for block in fars]
    x_near, x_far = arrange(at, even, odd)
    gradient = near_product(x_near, own, other)
    gradient, column_part, row_part = far_product(x_far, fars + others, gradient)
    column_state, sums = weigh(
        gradient, column_moment[None], copies(column_part, "col"), row_part
    )
    row_state, totals = totals_of(row_moment[None], copies(sums, ("dp", "row")))
    update, row_mean = clip(gradient, row_state, column_state, copies(totals, "col"))
    return (update, row_state[0], column_state[0], row_mean[0, 0])


def solution(mesh):
    return jax.shard_map(
        per_device,
        mesh=mesh,
        in_specs=(
            P(("dp", "row"), "col"),
            P(("dp", "col"), None, "row"),
            P("col"),
            P(("dp", "row")),
        ),
        out_specs=(P("col", ("dp", "row")), P("col"), P(("dp", "row")), P()),
        check_vma=False,
    )
```

```python
import jax
import jax.numpy as jnp
from jax import lax
from jax.experimental import pallas as pl
from jax.experimental.pallas import tpu as pltpu
from jax.sharding import PartitionSpec as P

D = 8192
FF = 32768
VMEM_LIMIT = 20 * 1024 * 1024
COLS = 512
REPLICAS = (0, 1, 2, 3)


def after_kernel(at_ref, *refs):
    for k in range(at_ref.shape[0]):
        refs[-1][k] = at_ref[k]


def after(at, *blocks):
    return pl.pallas_call(
        after_kernel,
        in_specs=[pl.BlockSpec(memory_space=pltpu.SMEM)]
        + [pl.BlockSpec(memory_space=pl.ANY)] * len(blocks),
        out_specs=pl.BlockSpec(memory_space=pltpu.SMEM),
        out_shape=jax.ShapeDtypeStruct(at.shape, at.dtype),
        cost_estimate=pl.CostEstimate(flops=1 << 34, bytes_accessed=0, transcendentals=0),
    )(at, *blocks)


def arrange_kernel(at_ref, even_ref, odd_ref, near_ref, far_ref):
    for far, out_ref in ((0, near_ref), (1, far_ref)):
        for other in (0, 1):
            for t in range(4):
                start = at_ref[t] + at_ref[4 + far] + at_ref[6 + other]
                rows = []
                for s in REPLICAS:
                    piece = odd_ref if s % 2 else even_ref
                    place = pl.multiple_of(start + s // 2 * 512, 32)
                    rows.append(piece[pl.ds(place, 32), :])
                column = other * 512 + t * 128
                out_ref[:, column : column + 128] = jnp.concatenate(rows, axis=0).T


def arrange(at, even, odd):
    whole = pl.BlockSpec(memory_space=pltpu.VMEM)
    return pl.pallas_call(
        arrange_kernel,
        in_specs=[pl.BlockSpec(memory_space=pltpu.SMEM), whole, whole],
        out_specs=[whole] * 2,
        out_shape=[jax.ShapeDtypeStruct((512, 1024), jnp.bfloat16)] * 2,
        compiler_params=PARAMS,
        cost_estimate=pl.CostEstimate(flops=0, bytes_accessed=4 << 20, transcendentals=0),
    )(at, even, odd)


def near_kernel(x_ref, own_ref, other_ref, out_ref):
    out_ref[...] = jnp.dot(
        x_ref[:, 0:512], own_ref[...], preferred_element_type=jnp.float32
    ) + jnp.dot(x_ref[:, 512:1024], other_ref[...], preferred_element_type=jnp.float32)


def across(value):
    part = value[:, 0:128]
    for k in range(1, COLS // 128):
        part = part + value[:, k * 128 : (k + 1) * 128]
    return part


def gather_rows(step, part, acc_ref, row_ref):
    @pl.when(step == 0)
    def _():
        acc_ref[...] = part

    @pl.when(step > 0)
    def _():
        acc_ref[...] += part

    @pl.when(step == pl.num_programs(0) - 1)
    def _():
        row_ref[...] = jnp.sum(acc_ref[...].T, axis=0, keepdims=True)


def far_kernel(x_ref, *refs):
    blocks, (near_ref, out_ref, col_ref, row_ref, acc_ref) = refs[:8], refs[8:]
    value = near_ref[...]
    for half in (0, 1):
        g = jnp.concatenate([ref[...] for ref in blocks[4 * half : 4 * half + 4]], axis=0)
        x = x_ref[:, 512 * half : 512 * half + 512]
        value += jnp.dot(x, g, preferred_element_type=jnp.float32)
    out_ref[...] = value
    squares = value * value + 1e-30
    col_ref[...] = jnp.sum(squares, axis=0, keepdims=True)
    gather_rows(pl.program_id(0), across(squares), acc_ref, row_ref)


def fixed(*shape):
    return pl.BlockSpec(shape, lambda j: (0, 0))


def moving(rows):
    return pl.BlockSpec((rows, COLS), lambda j: (0, j))


def in_vmem(value):
    return pltpu.with_memory_space_constraint(value, pltpu.VMEM)


G_SPEC = moving(512)
PARAMS = pltpu.CompilerParams(vmem_limit_bytes=VMEM_LIMIT)


COST = pl.CostEstimate(flops=2 * 512 * 1024 * 2048, bytes_accessed=9 << 20, transcendentals=0)


def near_product(x, own, other):
    return pl.pallas_call(
        near_kernel,
        grid=(2048 // COLS,),
        in_specs=[fixed(512, 1024), moving(512), moving(512)],
        out_specs=G_SPEC,
        out_shape=jax.ShapeDtypeStruct((512, 2048), jnp.float32),
        compiler_params=PARAMS,
        cost_estimate=COST,
    )(x, own, other)


def far_product(x, blocks, near):
    return pl.pallas_call(
        far_kernel,
        grid=(2048 // COLS,),
        in_specs=[fixed(512, 1024)] + [moving(128)] * 8 + [G_SPEC],
        out_specs=[G_SPEC, moving(1), fixed(1, 512)],
        out_shape=[
            pltpu.VMEM((512, 2048), jnp.float32),
            jax.ShapeDtypeStruct((1, 2048), jnp.float32),
            jax.ShapeDtypeStruct((1, 512), jnp.float32),
        ],
        scratch_shapes=[pltpu.VMEM((512, 128), jnp.float32)],
        compiler_params=PARAMS,
        cost_estimate=COST,
    )(x, *blocks, near)


def weigh_kernel(
    g_ref, moment_ref, parts_ref, row_ref, state_ref, copy_ref, out_ref, acc_ref, weighed_ref
):
    step = pl.program_id(0)
    sums = jnp.sum(parts_ref[...], axis=0, keepdims=True)
    state = 0.8 * moment_ref[...] + 0.2 * sums / D
    state_ref[...] = state
    copy_ref[...] = state
    scaled = g_ref[...] * lax.rsqrt(state)
    gather_rows(step, across(scaled * scaled), acc_ref, weighed_ref)

    @pl.when(step == pl.num_programs(0) - 1)
    def _():
        out_ref[:, 0:512] = row_ref[...]
        out_ref[:, 512:1024] = weighed_ref[...]


def weigh(g, column_moment, column_parts, row_part):
    return pl.pallas_call(
        weigh_kernel,
        grid=(2048 // COLS,),
        in_specs=[G_SPEC, moving(1), moving(16), fixed(1, 512)],
        out_specs=[moving(1), moving(1), fixed(1, 1024)],
        out_shape=[
            jax.ShapeDtypeStruct((1, 2048), jnp.float32),
            pltpu.VMEM((1, 2048), jnp.float32),
            jax.ShapeDtypeStruct((1, 1024), jnp.float32),
        ],
        scratch_shapes=[
            pltpu.VMEM((512, 128), jnp.float32),
            pltpu.VMEM((1, 512), jnp.float32),
        ],
        compiler_params=PARAMS,
        cost_estimate=pl.CostEstimate(
            flops=4 * 512 * 2048, bytes_accessed=4 << 20, transcendentals=0
        ),
    )(in_vmem(g), column_moment, column_parts, row_part)


def totals_kernel(moment_ref, parts_ref, state_ref, copy_ref, total_ref):
    sums = jnp.sum(parts_ref[...], axis=0, keepdims=True)
    state = 0.8 * moment_ref[...] + 0.2 * sums[:, 0:512] / FF
    state_ref[...] = state
    copy_ref[...] = state
    squares = jnp.sum(sums[:, 512:1024] / state)
    lane = lax.broadcasted_iota(jnp.int32, (1, 128), 1)
    total_ref[...] = jnp.where(lane == 0, squares, jnp.where(lane == 1, jnp.sum(state), 0.0))


def totals_of(row_moment, parts):
    return pl.pallas_call(
        totals_kernel,
        out_shape=[
            jax.ShapeDtypeStruct((1, 512), jnp.float32),
            pltpu.VMEM((1, 512), jnp.float32),
            jax.ShapeDtypeStruct((1, 128), jnp.float32),
        ],
        compiler_params=PARAMS,
        cost_estimate=pl.CostEstimate(flops=16384, bytes_accessed=70000, transcendentals=0),
    )(row_moment, parts)


def clip_kernel(g_ref, row_ref, col_ref, totals_ref, out_ref, mean_ref, rows_ref):
    @pl.when(pl.program_id(0) == 0)
    def _():
        rows_ref[...] = jnp.broadcast_to(lax.rsqrt(row_ref[...]), (128, 512)).T

    lane = lax.broadcasted_iota(jnp.int32, (1, 128), 1)
    totals = jnp.sum(totals_ref[...], axis=0, keepdims=True)
    total = jnp.sum(jnp.where(lane == 0, totals, 0.0), axis=1, keepdims=True)
    row_mean = jnp.sum(jnp.where(lane == 1, totals, 0.0), axis=1, keepdims=True) / D
    mean_ref[...] = row_mean
    clip_ratio = jnp.sqrt(row_mean * total / (D * FF))
    factor = jnp.sqrt(row_mean) / jnp.maximum(1.0, clip_ratio)
    columns = lax.rsqrt(col_ref[...]) * factor
    rows = rows_ref[...]
    for k in range(COLS // 128):
        piece = slice(k * 128, (k + 1) * 128)
        out_ref[:, piece] = g_ref[:, piece] * rows * columns[:, piece]


def clip(g, row_state, column_state, totals):
    return pl.pallas_call(
        clip_kernel,
        grid=(2048 // COLS,),
        in_specs=[G_SPEC, fixed(1, 512), moving(1), fixed(16, 128)],
        out_specs=[G_SPEC, fixed(1, 1)],
        out_shape=[
            jax.ShapeDtypeStruct((512, 2048), jnp.float32),
            jax.ShapeDtypeStruct((1, 1), jnp.float32),
        ],
        scratch_shapes=[pltpu.VMEM((512, 128), jnp.float32)],
        compiler_params=PARAMS,
        cost_estimate=pl.CostEstimate(
            flops=2 * 512 * 2048, bytes_accessed=8 << 20, transcendentals=0
        ),
    )(in_vmem(g), in_vmem(row_state), in_vmem(column_state), totals)


def cyclic(size, stride, shift):
    total = size * stride
    return [(j, (j + shift * stride) % total) for j in range(total)]


def flipped(total, mask):
    return [(j, j ^ mask) for j in range(total)]


def swap_cores(value):
    return lax.ppermute(value, "col", flipped(16, 1))


def swap_x(value, mask):
    return lax.ppermute(value, "dp", flipped(4, mask))


def move_y(value, shift):
    return lax.ppermute(value, "col", cyclic(4, 4, shift % 4))


def swap_row(value, mask):
    return lax.ppermute(value, "row", flipped(4, mask))


def swap_z(value):
    return lax.ppermute(value, "col", flipped(16, 2))


def copies(value, axis):
    rows = jnp.broadcast_to(value, (16,) + value.shape)
    return lax.all_to_all(rows, axis, 0, 0).reshape(16, value.shape[1])


def per_device(inputs, grad_out, row_moment, column_moment):
    me = lax.axis_index("dp")
    low = lax.axis_index("row")
    col = lax.axis_index("col")
    y, high, core = col // 4, col // 2 % 2, col % 2
    places = [low ^ ((y - t) % 4) for t in range(4)]
    starts = [(place % 2 * 2 + place // 2) * 128 for place in places]
    starts += [high * 64, (1 - high) * 64, core * 32, (1 - core) * 32]
    at = jnp.stack(starts).astype(jnp.int32)
    stage = lax.optimization_barrier

    pair = jnp.concatenate([inputs, swap_row(inputs, 2)])
    by_group = stage(jnp.transpose(grad_out, (1, 0, 2)))
    groups = [
        lax.dynamic_index_in_dim(by_group, me ^ s, 0, keepdims=False) for s in REPLICAS
    ]
    blocks = [groups[0]] + [swap_x(groups[s], s) for s in (1, 2, 3)]
    x0 = jnp.concatenate([pair, swap_row(pair, 1)])
    near, x0, at = stage((jnp.concatenate(blocks), x0, at))

    far = swap_z(near)
    nears = [move_y(near, t) for t in (1, 2, 3)]
    even = jnp.concatenate([x0, swap_x(x0, 2)])
    at = after(at, far)
    far, even, at, *nears = stage((far, even, at, *nears))

    own = jnp.concatenate([near, *nears])
    other = swap_cores(own)
    odd = swap_x(even, 1)
    fars = [move_y(far, t) for t in (1, 2, 3)]
    at = after(at, *fars)
    other, odd, at, far, *fars = stage((other, odd, at, far, *fars))

    fars = [far, *fars]
    others = [swap_cores(block) for block in fars]
    x_near, x_far = arrange(at, even, odd)
    gradient = near_product(x_near, own, other)
    gradient, column_part, row_part = far_product(x_far, fars + others, gradient)
    column_state, columns, sums = weigh(
        gradient, column_moment[None], copies(column_part, "col"), row_part
    )
    row_state, rows, totals = totals_of(row_moment[None], copies(sums, ("dp", "row")))
    update, row_mean = clip(gradient, rows, columns, copies(totals, "col"))
    return (update, row_state[0], column_state[0], row_mean[0, 0])


def solution(mesh):
    return jax.shard_map(
        per_device,
        mesh=mesh,
        in_specs=(
            P(("dp", "row"), "col"),
            P(("dp", "col"), None, "row"),
            P("col"),
            P(("dp", "row")),
        ),
        out_specs=(P("col", ("dp", "row")), P("col"), P(("dp", "row")), P()),
        check_vma=False,
    )
```

```python
import jax
import jax.numpy as jnp
from jax import lax
from jax.experimental import pallas as pl
from jax.experimental.pallas import tpu as pltpu
from jax.sharding import PartitionSpec as P

D = 8192
FF = 32768
VMEM_LIMIT = 20 * 1024 * 1024
COLS = 512
def after_kernel(value_ref, tile_ref, out_ref):
    del tile_ref
    out_ref[...] = value_ref[...]


def after(value, block):
    return pl.pallas_call(
        after_kernel,
        out_shape=jax.ShapeDtypeStruct(value.shape, value.dtype),
        cost_estimate=pl.CostEstimate(flops=1 << 34, bytes_accessed=0, transcendentals=0),
    )(value, block[0:16, 0:128])


def arrange_kernel(at_ref, *refs):
    pieces = refs[:4]
    for far, out_ref in enumerate(refs[4:]):
        for other in (0, 1):
            for t in range(4):
                start = pl.multiple_of(at_ref[t] + at_ref[4 + far] + at_ref[6 + other], 32)
                rows = [piece[pl.ds(start, 32), :] for piece in pieces]
                column = other * 512 + t * 128
                out_ref[:, column : column + 128] = jnp.concatenate(rows, axis=0).T


def arrange(at, pieces):
    whole = pl.BlockSpec(memory_space=pltpu.VMEM)
    return pl.pallas_call(
        arrange_kernel,
        in_specs=[pl.BlockSpec(memory_space=pltpu.SMEM)] + [whole] * 4,
        out_specs=[whole] * 2,
        out_shape=[jax.ShapeDtypeStruct((512, 1024), jnp.bfloat16)] * 2,
        compiler_params=PARAMS,
        cost_estimate=pl.CostEstimate(flops=0, bytes_accessed=4 << 20, transcendentals=0),
    )(at, *pieces)


def near_kernel(x_ref, own_ref, other_ref, out_ref):
    out_ref[...] = jnp.dot(
        x_ref[:, 0:512], own_ref[...], preferred_element_type=jnp.float32
    ) + jnp.dot(x_ref[:, 512:1024], other_ref[...], preferred_element_type=jnp.float32)


def across(value):
    part = value[:, 0:128]
    for k in range(1, COLS // 128):
        part = part + value[:, k * 128 : (k + 1) * 128]
    return part


def gather_rows(step, part, acc_ref, row_ref):
    @pl.when(step == 0)
    def _():
        acc_ref[...] = part

    @pl.when(step > 0)
    def _():
        acc_ref[...] += part

    @pl.when(step == pl.num_programs(0) - 1)
    def _():
        row_ref[...] = jnp.sum(acc_ref[...].T, axis=0, keepdims=True)


def far_kernel(x_ref, *refs):
    blocks, (near_ref, out_ref, col_ref, row_ref, acc_ref) = refs[:8], refs[8:]
    value = near_ref[...]
    for half in (0, 1):
        g = jnp.concatenate([ref[...] for ref in blocks[4 * half : 4 * half + 4]], axis=0)
        x = x_ref[:, 512 * half : 512 * half + 512]
        value += jnp.dot(x, g, preferred_element_type=jnp.float32)
    out_ref[...] = value
    squares = value * value + 1e-30
    col_ref[...] = jnp.sum(squares, axis=0, keepdims=True)
    gather_rows(pl.program_id(0), across(squares), acc_ref, row_ref)


def fixed(*shape):
    return pl.BlockSpec(shape, lambda j: (0, 0))


def moving(rows):
    return pl.BlockSpec((rows, COLS), lambda j: (0, j))


def in_vmem(value):
    return pltpu.with_memory_space_constraint(value, pltpu.VMEM)


G_SPEC = moving(512)
PARAMS = pltpu.CompilerParams(vmem_limit_bytes=VMEM_LIMIT)


COST = pl.CostEstimate(flops=2 * 512 * 1024 * 2048, bytes_accessed=9 << 20, transcendentals=0)


def near_product(x, own, other):
    return pl.pallas_call(
        near_kernel,
        grid=(2048 // COLS,),
        in_specs=[fixed(512, 1024), moving(512), moving(512)],
        out_specs=G_SPEC,
        out_shape=jax.ShapeDtypeStruct((512, 2048), jnp.float32),
        compiler_params=PARAMS,
        cost_estimate=COST,
    )(x, own, other)


def far_product(x, blocks, near):
    return pl.pallas_call(
        far_kernel,
        grid=(2048 // COLS,),
        in_specs=[fixed(512, 1024)] + [moving(128)] * 8 + [G_SPEC],
        out_specs=[G_SPEC, moving(1), fixed(1, 512)],
        out_shape=[
            pltpu.VMEM((512, 2048), jnp.float32),
            jax.ShapeDtypeStruct((1, 2048), jnp.float32),
            jax.ShapeDtypeStruct((1, 512), jnp.float32),
        ],
        scratch_shapes=[pltpu.VMEM((512, 128), jnp.float32)],
        compiler_params=PARAMS,
        cost_estimate=COST,
    )(x, *blocks, near)


def weigh_kernel(
    g_ref, moment_ref, parts_ref, row_ref, state_ref, copy_ref, out_ref, acc_ref, weighed_ref
):
    step = pl.program_id(0)
    sums = jnp.sum(parts_ref[...], axis=0, keepdims=True)
    state = 0.8 * moment_ref[...] + 0.2 * sums / D
    state_ref[...] = state
    copy_ref[...] = state
    scaled = g_ref[...] * lax.rsqrt(state)
    gather_rows(step, across(scaled * scaled), acc_ref, weighed_ref)

    @pl.when(step == pl.num_programs(0) - 1)
    def _():
        out_ref[:, 0:512] = row_ref[...]
        out_ref[:, 512:1024] = weighed_ref[...]


def weigh(g, column_moment, column_parts, row_part):
    return pl.pallas_call(
        weigh_kernel,
        grid=(2048 // COLS,),
        in_specs=[G_SPEC, moving(1), moving(16), fixed(1, 512)],
        out_specs=[moving(1), moving(1), fixed(1, 1024)],
        out_shape=[
            jax.ShapeDtypeStruct((1, 2048), jnp.float32),
            pltpu.VMEM((1, 2048), jnp.float32),
            jax.ShapeDtypeStruct((1, 1024), jnp.float32),
        ],
        scratch_shapes=[
            pltpu.VMEM((512, 128), jnp.float32),
            pltpu.VMEM((1, 512), jnp.float32),
        ],
        compiler_params=PARAMS,
        cost_estimate=pl.CostEstimate(
            flops=4 * 512 * 2048, bytes_accessed=4 << 20, transcendentals=0
        ),
    )(in_vmem(g), column_moment, column_parts, row_part)


def totals_kernel(moment_ref, parts_ref, state_ref, copy_ref, total_ref):
    sums = jnp.sum(parts_ref[...], axis=0, keepdims=True)
    state = 0.8 * moment_ref[...] + 0.2 * sums[:, 0:512] / FF
    state_ref[...] = state
    copy_ref[...] = state
    squares = jnp.sum(sums[:, 512:1024] / state)
    lane = lax.broadcasted_iota(jnp.int32, (1, 128), 1)
    total_ref[...] = jnp.where(lane == 0, squares, jnp.where(lane == 1, jnp.sum(state), 0.0))


def totals_of(row_moment, parts):
    return pl.pallas_call(
        totals_kernel,
        out_shape=[
            jax.ShapeDtypeStruct((1, 512), jnp.float32),
            pltpu.VMEM((1, 512), jnp.float32),
            jax.ShapeDtypeStruct((1, 128), jnp.float32),
        ],
        compiler_params=PARAMS,
        cost_estimate=pl.CostEstimate(flops=16384, bytes_accessed=70000, transcendentals=0),
    )(row_moment, parts)


def clip_kernel(g_ref, row_ref, col_ref, totals_ref, out_ref, mean_ref, rows_ref):
    @pl.when(pl.program_id(0) == 0)
    def _():
        rows_ref[...] = jnp.broadcast_to(lax.rsqrt(row_ref[...]), (128, 512)).T

    lane = lax.broadcasted_iota(jnp.int32, (1, 128), 1)
    totals = jnp.sum(totals_ref[...], axis=0, keepdims=True)
    total = jnp.sum(jnp.where(lane == 0, totals, 0.0), axis=1, keepdims=True)
    row_mean = jnp.sum(jnp.where(lane == 1, totals, 0.0), axis=1, keepdims=True) / D
    mean_ref[...] = row_mean
    clip_ratio = jnp.sqrt(row_mean * total / (D * FF))
    factor = jnp.sqrt(row_mean) / jnp.maximum(1.0, clip_ratio)
    columns = lax.rsqrt(col_ref[...]) * factor
    rows = rows_ref[...]
    for k in range(COLS // 128):
        piece = slice(k * 128, (k + 1) * 128)
        out_ref[:, piece] = g_ref[:, piece] * rows * columns[:, piece]


def clip(g, row_state, column_state, totals):
    return pl.pallas_call(
        clip_kernel,
        grid=(2048 // COLS,),
        in_specs=[G_SPEC, fixed(1, 512), moving(1), fixed(16, 128)],
        out_specs=[G_SPEC, fixed(1, 1)],
        out_shape=[
            jax.ShapeDtypeStruct((512, 2048), jnp.float32),
            jax.ShapeDtypeStruct((1, 1), jnp.float32),
        ],
        scratch_shapes=[pltpu.VMEM((512, 128), jnp.float32)],
        compiler_params=PARAMS,
        cost_estimate=pl.CostEstimate(
            flops=2 * 512 * 2048, bytes_accessed=8 << 20, transcendentals=0
        ),
    )(in_vmem(g), in_vmem(row_state), in_vmem(column_state), totals)


def cyclic(size, stride, shift):
    total = size * stride
    return [(j, (j + shift * stride) % total) for j in range(total)]


def flipped(total, mask):
    return [(j, j ^ mask) for j in range(total)]


def swap_cores(value):
    return lax.ppermute(value, "col", flipped(16, 1))


def swap_x(value, mask):
    return lax.ppermute(value, "dp", flipped(4, mask))


def move_y(value, shift):
    return lax.ppermute(value, "col", cyclic(4, 4, shift % 4))


def swap_row(value, mask):
    return lax.ppermute(value, "row", flipped(4, mask))


def swap_z(value):
    return lax.ppermute(value, "col", flipped(16, 2))


def copies(value, axis):
    rows = jnp.broadcast_to(value, (16,) + value.shape)
    return lax.all_to_all(rows, axis, 0, 0).reshape(16, value.shape[1])


def per_device(inputs, grad_out, row_moment, column_moment):
    me = lax.axis_index("dp")
    low = lax.axis_index("row")
    col = lax.axis_index("col")
    y, high, core = col // 4, col // 2 % 2, col % 2
    places = [low ^ ((y - t) % 4) for t in range(4)]
    starts = [(place % 2 * 2 + place // 2) * 128 for place in places]
    starts += [high * 64, (1 - high) * 64, core * 32, (1 - core) * 32]
    at = jnp.stack(starts).astype(jnp.int32)
    stage = lax.optimization_barrier

    pair = jnp.concatenate([inputs, swap_row(inputs, 2)])
    by_group = stage(jnp.transpose(grad_out, (1, 0, 2)))
    groups = [
        lax.dynamic_index_in_dim(by_group, me ^ s, 0, keepdims=False) for s in range(4)
    ]
    blocks = [groups[0]] + [swap_x(groups[s], s) for s in (1, 2, 3)]
    x0 = jnp.concatenate([pair, swap_row(pair, 1)])
    near, x0, at = stage((jnp.concatenate(blocks), x0, at))

    far = swap_z(near)
    nears = [move_y(near, t) for t in (1, 2, 3)]
    x2 = swap_x(x0, 2)
    moment = after(column_moment[None], far)
    far, moment, x0, x2, *nears = stage((far, moment, x0, x2, *nears))

    own = jnp.concatenate([near, *nears])
    other = swap_cores(own)
    x1, x3 = swap_x(x0, 1), swap_x(x0, 3)
    fars = [move_y(far, t) for t in (1, 2, 3)]
    x_near, x_far = arrange(at, (x0, x1, x2, x3))
    other, x_near, x_far, far, *fars = stage((other, x_near, x_far, far, *fars))

    fars = [far, *fars]
    others = [swap_cores(block) for block in fars]
    gradient = near_product(x_near, own, other)
    gradient, column_part, row_part = far_product(x_far, fars + others, gradient)
    column_state, columns, sums = weigh(
        gradient, moment, copies(column_part, "col"), row_part
    )
    row_state, rows, totals = totals_of(row_moment[None], copies(sums, ("dp", "row")))
    update, row_mean = clip(gradient, rows, columns, copies(totals, "col"))
    return (update, row_state[0], column_state[0], row_mean[0, 0])


def solution(mesh):
    return jax.shard_map(
        per_device,
        mesh=mesh,
        in_specs=(
            P(("dp", "row"), "col"),
            P(("dp", "col"), None, "row"),
            P("col"),
            P(("dp", "row")),
        ),
        out_specs=(P("col", ("dp", "row")), P("col"), P(("dp", "row")), P()),
        check_vma=False,
    )
```

```python
import jax
import jax.numpy as jnp
from jax import lax
from jax.experimental import pallas as pl
from jax.experimental.pallas import tpu as pltpu
from jax.sharding import PartitionSpec as P

D = 8192
FF = 32768
VMEM_LIMIT = 20 * 1024 * 1024
COLS = 512
def after_kernel(*refs):
    refs[-1][...] = jnp.zeros_like(refs[-1])


def after(*blocks):
    return pl.pallas_call(
        after_kernel,
        in_specs=[pl.BlockSpec(memory_space=pl.ANY)] * len(blocks),
        out_shape=pltpu.VMEM((8, 128), jnp.float32),
        cost_estimate=pl.CostEstimate(flops=1 << 34, bytes_accessed=0, transcendentals=0),
    )(*blocks)


def arrange_kernel(at_ref, *refs):
    pieces = refs[:4]
    for far, out_ref in enumerate(refs[4:]):
        for other in (0, 1):
            for t in range(4):
                start = pl.multiple_of(at_ref[t] + at_ref[4 + far] + at_ref[6 + other], 32)
                rows = [piece[pl.ds(start, 32), :] for piece in pieces]
                column = other * 512 + t * 128
                out_ref[:, column : column + 128] = jnp.concatenate(rows, axis=0).T


def arrange(at, pieces):
    whole = pl.BlockSpec(memory_space=pltpu.VMEM)
    return pl.pallas_call(
        arrange_kernel,
        in_specs=[pl.BlockSpec(memory_space=pltpu.SMEM)] + [whole] * 4,
        out_specs=[whole] * 2,
        out_shape=[jax.ShapeDtypeStruct((512, 1024), jnp.bfloat16)] * 2,
        compiler_params=PARAMS,
        cost_estimate=pl.CostEstimate(flops=0, bytes_accessed=4 << 20, transcendentals=0),
    )(at, *pieces)


def near_kernel(x_ref, own_ref, other_ref, first_ref, second_ref, out_ref):
    del first_ref, second_ref
    out_ref[...] = jnp.dot(
        x_ref[:, 0:512], own_ref[...], preferred_element_type=jnp.float32
    ) + jnp.dot(x_ref[:, 512:1024], other_ref[...], preferred_element_type=jnp.float32)


def across(value):
    part = value[:, 0:128]
    for k in range(1, COLS // 128):
        part = part + value[:, k * 128 : (k + 1) * 128]
    return part


def gather_rows(step, part, acc_ref, row_ref):
    @pl.when(step == 0)
    def _():
        acc_ref[...] = part

    @pl.when(step > 0)
    def _():
        acc_ref[...] += part

    @pl.when(step == pl.num_programs(0) - 1)
    def _():
        row_ref[...] = jnp.sum(acc_ref[...].T, axis=0, keepdims=True)


def far_kernel(x_ref, *refs):
    blocks, (near_ref, out_ref, col_ref, row_ref, acc_ref) = refs[:8], refs[8:]
    value = near_ref[...]
    for half in (0, 1):
        g = jnp.concatenate([ref[...] for ref in blocks[4 * half : 4 * half + 4]], axis=0)
        x = x_ref[:, 512 * half : 512 * half + 512]
        value += jnp.dot(x, g, preferred_element_type=jnp.float32)
    out_ref[...] = value
    squares = value * value + 1e-30
    col_ref[...] = jnp.sum(squares, axis=0, keepdims=True)
    gather_rows(pl.program_id(0), across(squares), acc_ref, row_ref)


def fixed(*shape):
    return pl.BlockSpec(shape, lambda j: (0, 0))


def moving(rows):
    return pl.BlockSpec((rows, COLS), lambda j: (0, j))


def in_vmem(value):
    return pltpu.with_memory_space_constraint(value, pltpu.VMEM)


G_SPEC = moving(512)
PARAMS = pltpu.CompilerParams(vmem_limit_bytes=VMEM_LIMIT)


COST = pl.CostEstimate(flops=2 * 512 * 1024 * 2048, bytes_accessed=9 << 20, transcendentals=0)


def near_product(x, own, other, tokens):
    return pl.pallas_call(
        near_kernel,
        grid=(2048 // COLS,),
        in_specs=[fixed(512, 1024), moving(512), moving(512), fixed(8, 128), fixed(8, 128)],
        out_specs=G_SPEC,
        out_shape=jax.ShapeDtypeStruct((512, 2048), jnp.float32),
        compiler_params=PARAMS,
        cost_estimate=COST,
    )(x, own, other, *tokens)


def far_product(x, blocks, near):
    return pl.pallas_call(
        far_kernel,
        grid=(2048 // COLS,),
        in_specs=[fixed(512, 1024)] + [moving(128)] * 8 + [G_SPEC],
        out_specs=[G_SPEC, moving(1), fixed(1, 512)],
        out_shape=[
            pltpu.VMEM((512, 2048), jnp.float32),
            jax.ShapeDtypeStruct((1, 2048), jnp.float32),
            jax.ShapeDtypeStruct((1, 512), jnp.float32),
        ],
        scratch_shapes=[pltpu.VMEM((512, 128), jnp.float32)],
        compiler_params=PARAMS,
        cost_estimate=COST,
    )(x, *blocks, near)


def weigh_kernel(
    g_ref, moment_ref, parts_ref, row_ref, state_ref, copy_ref, out_ref, acc_ref, weighed_ref
):
    step = pl.program_id(0)
    sums = jnp.sum(parts_ref[...], axis=0, keepdims=True)
    state = 0.8 * moment_ref[...] + 0.2 * sums / D
    state_ref[...] = state
    copy_ref[...] = state
    scaled = g_ref[...] * lax.rsqrt(state)
    gather_rows(step, across(scaled * scaled), acc_ref, weighed_ref)

    @pl.when(step == pl.num_programs(0) - 1)
    def _():
        out_ref[:, 0:512] = row_ref[...]
        out_ref[:, 512:1024] = weighed_ref[...]


def weigh(g, column_moment, column_parts, row_part):
    return pl.pallas_call(
        weigh_kernel,
        grid=(2048 // COLS,),
        in_specs=[G_SPEC, moving(1), moving(16), fixed(1, 512)],
        out_specs=[moving(1), moving(1), fixed(1, 1024)],
        out_shape=[
            jax.ShapeDtypeStruct((1, 2048), jnp.float32),
            pltpu.VMEM((1, 2048), jnp.float32),
            jax.ShapeDtypeStruct((1, 1024), jnp.float32),
        ],
        scratch_shapes=[
            pltpu.VMEM((512, 128), jnp.float32),
            pltpu.VMEM((1, 512), jnp.float32),
        ],
        compiler_params=PARAMS,
        cost_estimate=pl.CostEstimate(
            flops=4 * 512 * 2048, bytes_accessed=4 << 20, transcendentals=0
        ),
    )(in_vmem(g), column_moment, column_parts, row_part)


def totals_kernel(moment_ref, parts_ref, state_ref, copy_ref, total_ref):
    sums = jnp.sum(parts_ref[...], axis=0, keepdims=True)
    state = 0.8 * moment_ref[...] + 0.2 * sums[:, 0:512] / FF
    state_ref[...] = state
    copy_ref[...] = state
    squares = jnp.sum(sums[:, 512:1024] / state)
    lane = lax.broadcasted_iota(jnp.int32, (1, 128), 1)
    total_ref[...] = jnp.where(lane == 0, squares, jnp.where(lane == 1, jnp.sum(state), 0.0))


def totals_of(row_moment, parts):
    return pl.pallas_call(
        totals_kernel,
        out_shape=[
            jax.ShapeDtypeStruct((1, 512), jnp.float32),
            pltpu.VMEM((1, 512), jnp.float32),
            jax.ShapeDtypeStruct((1, 128), jnp.float32),
        ],
        compiler_params=PARAMS,
        cost_estimate=pl.CostEstimate(flops=16384, bytes_accessed=70000, transcendentals=0),
    )(row_moment, parts)


def clip_kernel(g_ref, row_ref, col_ref, totals_ref, out_ref, mean_ref, rows_ref):
    @pl.when(pl.program_id(0) == 0)
    def _():
        rows_ref[...] = jnp.broadcast_to(lax.rsqrt(row_ref[...]), (128, 512)).T

    lane = lax.broadcasted_iota(jnp.int32, (1, 128), 1)
    totals = jnp.sum(totals_ref[...], axis=0, keepdims=True)
    total = jnp.sum(jnp.where(lane == 0, totals, 0.0), axis=1, keepdims=True)
    row_mean = jnp.sum(jnp.where(lane == 1, totals, 0.0), axis=1, keepdims=True) / D
    mean_ref[...] = row_mean
    clip_ratio = jnp.sqrt(row_mean * total / (D * FF))
    factor = jnp.sqrt(row_mean) / jnp.maximum(1.0, clip_ratio)
    columns = lax.rsqrt(col_ref[...]) * factor
    rows = rows_ref[...]
    for k in range(COLS // 128):
        piece = slice(k * 128, (k + 1) * 128)
        out_ref[:, piece] = g_ref[:, piece] * rows * columns[:, piece]


def clip(g, row_state, column_state, totals):
    return pl.pallas_call(
        clip_kernel,
        grid=(2048 // COLS,),
        in_specs=[G_SPEC, fixed(1, 512), moving(1), fixed(16, 128)],
        out_specs=[G_SPEC, fixed(1, 1)],
        out_shape=[
            jax.ShapeDtypeStruct((512, 2048), jnp.float32),
            jax.ShapeDtypeStruct((1, 1), jnp.float32),
        ],
        scratch_shapes=[pltpu.VMEM((512, 128), jnp.float32)],
        compiler_params=PARAMS,
        cost_estimate=pl.CostEstimate(
            flops=2 * 512 * 2048, bytes_accessed=8 << 20, transcendentals=0
        ),
    )(in_vmem(g), in_vmem(row_state), in_vmem(column_state), totals)


def cyclic(size, stride, shift):
    total = size * stride
    return [(j, (j + shift * stride) % total) for j in range(total)]


def flipped(total, mask):
    return [(j, j ^ mask) for j in range(total)]


def swap_cores(value):
    return lax.ppermute(value, "col", flipped(16, 1))


def swap_x(value, mask):
    return lax.ppermute(value, "dp", flipped(4, mask))


def move_y(value, shift):
    return lax.ppermute(value, "col", cyclic(4, 4, shift % 4))


def swap_row(value, mask):
    return lax.ppermute(value, "row", flipped(4, mask))


def swap_z(value):
    return lax.ppermute(value, "col", flipped(16, 2))


def copies(value, axis):
    rows = jnp.broadcast_to(value, (16,) + value.shape)
    return lax.all_to_all(rows, axis, 0, 0).reshape(16, value.shape[1])


def per_device(inputs, grad_out, row_moment, column_moment):
    me = lax.axis_index("dp")
    low = lax.axis_index("row")
    col = lax.axis_index("col")
    y, high, core = col // 4, col // 2 % 2, col % 2
    places = [low ^ ((y - t) % 4) for t in range(4)]
    starts = [(place % 2 * 2 + place // 2) * 128 for place in places]
    starts += [high * 64, (1 - high) * 64, core * 32, (1 - core) * 32]
    at = jnp.stack(starts).astype(jnp.int32)
    stage = lax.optimization_barrier

    pair = jnp.concatenate([inputs, swap_row(inputs, 2)])
    by_group = stage(jnp.transpose(grad_out, (1, 0, 2)))
    groups = [
        lax.dynamic_index_in_dim(by_group, me ^ s, 0, keepdims=False) for s in range(4)
    ]
    blocks = [groups[0]] + [swap_x(groups[s], s) for s in (1, 2, 3)]
    x0 = jnp.concatenate([pair, swap_row(pair, 1)])
    near, x0, at = stage((jnp.concatenate(blocks), x0, at))

    far = swap_z(near)
    nears = [move_y(near, t) for t in (1, 2, 3)]
    x2 = swap_x(x0, 2)
    early = after(far)
    far, early, x0, x2, *nears = stage((far, early, x0, x2, *nears))

    own = jnp.concatenate([near, *nears])
    other = swap_cores(own)
    x1, x3 = swap_x(x0, 1), swap_x(x0, 3)
    fars = [move_y(far, t) for t in (1, 2, 3)]
    x_near, x_far = arrange(at, (x0, x1, x2, x3))
    late = after(*fars)
    late, x_near, x_far, far, *fars = stage((late, x_near, x_far, far, *fars))

    fars = [far, *fars]
    others = [swap_cores(block) for block in fars]
    gradient = near_product(x_near, own, other, (early, late))
    gradient, column_part, row_part = far_product(x_far, fars + others, gradient)
    column_state, columns, sums = weigh(
        gradient, column_moment[None], copies(column_part, "col"), row_part
    )
    row_state, rows, totals = totals_of(row_moment[None], copies(sums, ("dp", "row")))
    update, row_mean = clip(gradient, rows, columns, copies(totals, "col"))
    return (update, row_state[0], column_state[0], row_mean[0, 0])


def solution(mesh):
    return jax.shard_map(
        per_device,
        mesh=mesh,
        in_specs=(
            P(("dp", "row"), "col"),
            P(("dp", "col"), None, "row"),
            P("col"),
            P(("dp", "row")),
        ),
        out_specs=(P("col", ("dp", "row")), P("col"), P(("dp", "row")), P()),
        check_vma=False,
    )
```

```python
import jax
import jax.numpy as jnp
from jax import lax
from jax.experimental import pallas as pl
from jax.experimental.pallas import tpu as pltpu
from jax.sharding import PartitionSpec as P

D = 8192
FF = 32768
VMEM_LIMIT = 20 * 1024 * 1024
COLS = 512
def after_kernel(*refs):
    refs[-1][...] = jnp.zeros_like(refs[-1])


def after(*blocks, scale=34):
    return pl.pallas_call(
        after_kernel,
        in_specs=[pl.BlockSpec(memory_space=pl.ANY)] * len(blocks),
        out_shape=pltpu.VMEM((8, 128), jnp.float32),
        cost_estimate=pl.CostEstimate(flops=1 << scale, bytes_accessed=0, transcendentals=0),
    )(*blocks)


NEAR = [(s, t, far) for t in range(4) for s, far in ((0, 0), (1, 0), (2, 0), (3, 0), (0, 1))]
FAR = [(s, t, 1) for t in range(4) for s in (1, 2, 3)]


def arrange_kernel(at_ref, *refs):
    pieces = refs[:4]
    for order, out_ref in zip((NEAR, FAR), refs[4:]):
        blocks = [block + (other,) for other in (0, 1) for block in order]
        for k in range(0, len(blocks), 4):
            rows = []
            for s, t, far, other in blocks[k : k + 4]:
                start = pl.multiple_of(at_ref[t] + at_ref[4 + far] + at_ref[6 + other], 32)
                rows.append(pieces[s][pl.ds(start, 32), :])
            out_ref[:, 32 * k : 32 * k + 128] = jnp.concatenate(rows, axis=0).T


def arrange(at, pieces):
    whole = pl.BlockSpec(memory_space=pltpu.VMEM)
    return pl.pallas_call(
        arrange_kernel,
        in_specs=[pl.BlockSpec(memory_space=pltpu.SMEM)] + [whole] * 4,
        out_specs=[whole] * 2,
        out_shape=[
            jax.ShapeDtypeStruct((512, 64 * len(order)), jnp.bfloat16) for order in (NEAR, FAR)
        ],
        compiler_params=PARAMS,
        cost_estimate=pl.CostEstimate(flops=0, bytes_accessed=4 << 20, transcendentals=0),
    )(at, *pieces)


def near_kernel(x_ref, own_ref, other_ref, first_ref, second_ref, out_ref):
    del first_ref, second_ref
    out_ref[...] = jnp.dot(
        x_ref[:, 0:640], own_ref[...], preferred_element_type=jnp.float32
    ) + jnp.dot(x_ref[:, 640:1280], other_ref[...], preferred_element_type=jnp.float32)


def across(value):
    part = value[:, 0:128]
    for k in range(1, COLS // 128):
        part = part + value[:, k * 128 : (k + 1) * 128]
    return part


def gather_rows(step, part, acc_ref, row_ref):
    @pl.when(step == 0)
    def _():
        acc_ref[...] = part

    @pl.when(step > 0)
    def _():
        acc_ref[...] += part

    @pl.when(step == pl.num_programs(0) - 1)
    def _():
        row_ref[...] = jnp.sum(acc_ref[...].T, axis=0, keepdims=True)


def far_kernel(x_ref, *refs):
    blocks, (near_ref, out_ref, col_ref, row_ref, acc_ref) = refs[:8], refs[8:]
    value = near_ref[...]
    for half in (0, 1):
        g = jnp.concatenate([ref[...] for ref in blocks[4 * half : 4 * half + 4]], axis=0)
        x = x_ref[:, 384 * half : 384 * half + 384]
        value += jnp.dot(x, g, preferred_element_type=jnp.float32)
    out_ref[...] = value
    squares = value * value + 1e-30
    col_ref[...] = jnp.sum(squares, axis=0, keepdims=True)
    gather_rows(pl.program_id(0), across(squares), acc_ref, row_ref)


def fixed(*shape):
    return pl.BlockSpec(shape, lambda j: (0, 0))


def moving(rows):
    return pl.BlockSpec((rows, COLS), lambda j: (0, j))


def in_vmem(value):
    return pltpu.with_memory_space_constraint(value, pltpu.VMEM)


G_SPEC = moving(512)
PARAMS = pltpu.CompilerParams(vmem_limit_bytes=VMEM_LIMIT)


COST = pl.CostEstimate(flops=2 * 512 * 1024 * 2048, bytes_accessed=9 << 20, transcendentals=0)


def near_product(x, own, other, tokens):
    return pl.pallas_call(
        near_kernel,
        grid=(2048 // COLS,),
        in_specs=[fixed(512, 1280), moving(640), moving(640), fixed(8, 128), fixed(8, 128)],
        out_specs=G_SPEC,
        out_shape=jax.ShapeDtypeStruct((512, 2048), jnp.float32),
        compiler_params=PARAMS,
        cost_estimate=COST,
    )(x, own, other, *tokens)


def far_product(x, blocks, near):
    return pl.pallas_call(
        far_kernel,
        grid=(2048 // COLS,),
        in_specs=[fixed(512, 768)] + [moving(96)] * 8 + [G_SPEC],
        out_specs=[G_SPEC, moving(1), fixed(1, 512)],
        out_shape=[
            pltpu.VMEM((512, 2048), jnp.float32),
            jax.ShapeDtypeStruct((1, 2048), jnp.float32),
            jax.ShapeDtypeStruct((1, 512), jnp.float32),
        ],
        scratch_shapes=[pltpu.VMEM((512, 128), jnp.float32)],
        compiler_params=PARAMS,
        cost_estimate=COST,
    )(x, *blocks, near)


def weigh_kernel(
    g_ref, moment_ref, parts_ref, row_ref, state_ref, copy_ref, out_ref, acc_ref, weighed_ref
):
    step = pl.program_id(0)
    sums = jnp.sum(parts_ref[...], axis=0, keepdims=True)
    state = 0.8 * moment_ref[...] + 0.2 * sums / D
    state_ref[...] = state
    copy_ref[...] = state
    scaled = g_ref[...] * lax.rsqrt(state)
    gather_rows(step, across(scaled * scaled), acc_ref, weighed_ref)

    @pl.when(step == pl.num_programs(0) - 1)
    def _():
        out_ref[:, 0:512] = row_ref[...]
        out_ref[:, 512:1024] = weighed_ref[...]


def weigh(g, column_moment, column_parts, row_part):
    return pl.pallas_call(
        weigh_kernel,
        grid=(2048 // COLS,),
        in_specs=[G_SPEC, moving(1), moving(16), fixed(1, 512)],
        out_specs=[moving(1), moving(1), fixed(1, 1024)],
        out_shape=[
            jax.ShapeDtypeStruct((1, 2048), jnp.float32),
            pltpu.VMEM((1, 2048), jnp.float32),
            jax.ShapeDtypeStruct((1, 1024), jnp.float32),
        ],
        scratch_shapes=[
            pltpu.VMEM((512, 128), jnp.float32),
            pltpu.VMEM((1, 512), jnp.float32),
        ],
        compiler_params=PARAMS,
        cost_estimate=pl.CostEstimate(
            flops=4 * 512 * 2048, bytes_accessed=4 << 20, transcendentals=0
        ),
    )(in_vmem(g), column_moment, column_parts, row_part)


def totals_kernel(moment_ref, parts_ref, state_ref, copy_ref, total_ref):
    sums = jnp.sum(parts_ref[...], axis=0, keepdims=True)
    state = 0.8 * moment_ref[...] + 0.2 * sums[:, 0:512] / FF
    state_ref[...] = state
    copy_ref[...] = state
    squares = jnp.sum(sums[:, 512:1024] / state)
    lane = lax.broadcasted_iota(jnp.int32, (1, 128), 1)
    total_ref[...] = jnp.where(lane == 0, squares, jnp.where(lane == 1, jnp.sum(state), 0.0))


def totals_of(row_moment, parts):
    return pl.pallas_call(
        totals_kernel,
        out_shape=[
            jax.ShapeDtypeStruct((1, 512), jnp.float32),
            pltpu.VMEM((1, 512), jnp.float32),
            jax.ShapeDtypeStruct((1, 128), jnp.float32),
        ],
        compiler_params=PARAMS,
        cost_estimate=pl.CostEstimate(flops=16384, bytes_accessed=70000, transcendentals=0),
    )(row_moment, parts)


def clip_kernel(g_ref, row_ref, col_ref, totals_ref, out_ref, mean_ref, rows_ref):
    @pl.when(pl.program_id(0) == 0)
    def _():
        rows_ref[...] = jnp.broadcast_to(lax.rsqrt(row_ref[...]), (128, 512)).T

    lane = lax.broadcasted_iota(jnp.int32, (1, 128), 1)
    totals = jnp.sum(totals_ref[...], axis=0, keepdims=True)
    total = jnp.sum(jnp.where(lane == 0, totals, 0.0), axis=1, keepdims=True)
    row_mean = jnp.sum(jnp.where(lane == 1, totals, 0.0), axis=1, keepdims=True) / D
    mean_ref[...] = row_mean
    clip_ratio = jnp.sqrt(row_mean * total / (D * FF))
    factor = jnp.sqrt(row_mean) / jnp.maximum(1.0, clip_ratio)
    columns = lax.rsqrt(col_ref[...]) * factor
    rows = rows_ref[...]
    for k in range(COLS // 128):
        piece = slice(k * 128, (k + 1) * 128)
        out_ref[:, piece] = g_ref[:, piece] * rows * columns[:, piece]


def clip(g, row_state, column_state, totals):
    return pl.pallas_call(
        clip_kernel,
        grid=(2048 // COLS,),
        in_specs=[G_SPEC, fixed(1, 512), moving(1), fixed(16, 128)],
        out_specs=[G_SPEC, fixed(1, 1)],
        out_shape=[
            jax.ShapeDtypeStruct((512, 2048), jnp.float32),
            jax.ShapeDtypeStruct((1, 1), jnp.float32),
        ],
        scratch_shapes=[pltpu.VMEM((512, 128), jnp.float32)],
        compiler_params=PARAMS,
        cost_estimate=pl.CostEstimate(
            flops=2 * 512 * 2048, bytes_accessed=8 << 20, transcendentals=0
        ),
    )(in_vmem(g), in_vmem(row_state), in_vmem(column_state), totals)


def cyclic(size, stride, shift):
    total = size * stride
    return [(j, (j + shift * stride) % total) for j in range(total)]


def flipped(total, mask):
    return [(j, j ^ mask) for j in range(total)]


def swap_cores(value):
    return lax.ppermute(value, "col", flipped(16, 1))


def swap_x(value, mask):
    return lax.ppermute(value, "dp", flipped(4, mask))


def move_y(value, shift):
    return lax.ppermute(value, "col", cyclic(4, 4, shift % 4))


def swap_row(value, mask):
    return lax.ppermute(value, "row", flipped(4, mask))


def swap_z(value):
    return lax.ppermute(value, "col", flipped(16, 2))


def copies(value, axis):
    rows = jnp.broadcast_to(value, (16,) + value.shape)
    return lax.all_to_all(rows, axis, 0, 0).reshape(16, value.shape[1])


def per_device(inputs, grad_out, row_moment, column_moment):
    me = lax.axis_index("dp")
    low = lax.axis_index("row")
    col = lax.axis_index("col")
    y, high, core = col // 4, col // 2 % 2, col % 2
    places = [low ^ ((y - t) % 4) for t in range(4)]
    starts = [(place % 2 * 2 + place // 2) * 128 for place in places]
    starts += [high * 64, (1 - high) * 64, core * 32, (1 - core) * 32]
    at = jnp.stack(starts).astype(jnp.int32)
    stage = lax.optimization_barrier

    pair = jnp.concatenate([inputs, swap_row(inputs, 2)])
    by_group = stage(jnp.transpose(grad_out, (1, 0, 2)))
    groups = [
        lax.dynamic_index_in_dim(by_group, me ^ s, 0, keepdims=False) for s in range(4)
    ]
    far0 = swap_z(groups[0])
    blocks = [swap_x(groups[s], s) for s in (1, 2, 3)]
    near = jnp.concatenate([groups[0]] + blocks + [far0])
    near, rest, pair, at = stage((near, jnp.concatenate(blocks), pair, at))

    far = swap_z(rest)
    near1, near3 = move_y(near, 1), move_y(near, -1)
    x0 = jnp.concatenate([pair, swap_row(pair, 1)])
    near1, near3, x0 = stage((near1, near3, x0))
    near2a, near2b = move_y(near1[0:80], 1), move_y(near3[80:160], -1)
    x1, x3 = swap_x(x0, 1), swap_x(x0, 3)
    early = after(far)
    far, early, x0, x1, x3, near2a, near2b = stage((far, early, x0, x1, x3, near2a, near2b))

    own = jnp.concatenate([near, near1, near2a, near2b, near3])
    other = swap_cores(own)
    x2 = swap_x(x0, 2)
    fars = [move_y(far, t) for t in (1, 2, 3)]
    x_near, x_far = arrange(at, (x0, x1, x2, x3))
    late = after(x_far, *fars, scale=35)
    late, x_near, x_far, far, *fars = stage((late, x_near, x_far, far, *fars))

    fars = [far, *fars]
    others = [swap_cores(block) for block in fars]
    gradient = near_product(x_near, own, other, (early, late))
    gradient, column_part, row_part = far_product(x_far, fars + others, gradient)
    column_state, columns, sums = weigh(
        gradient, column_moment[None], copies(column_part, "col"), row_part
    )
    row_state, rows, totals = totals_of(row_moment[None], copies(sums, ("dp", "row")))
    update, row_mean = clip(gradient, rows, columns, copies(totals, "col"))
    return (update, row_state[0], column_state[0], row_mean[0, 0])


def solution(mesh):
    return jax.shard_map(
        per_device,
        mesh=mesh,
        in_specs=(
            P(("dp", "row"), "col"),
            P(("dp", "col"), None, "row"),
            P("col"),
            P(("dp", "row")),
        ),
        out_specs=(P("col", ("dp", "row")), P("col"), P(("dp", "row")), P()),
        check_vma=False,
    )
```

```python
import jax
import jax.numpy as jnp
from jax import lax
from jax.experimental import pallas as pl
from jax.experimental.pallas import tpu as pltpu
from jax.sharding import PartitionSpec as P

D = 8192
FF = 32768
VMEM_LIMIT = 20 * 1024 * 1024
COLS = 512
def after_kernel(*refs):
    refs[-1][...] = jnp.zeros_like(refs[-1])


def after(*blocks, scale=34):
    return pl.pallas_call(
        after_kernel,
        in_specs=[pl.BlockSpec(memory_space=pl.ANY)] * len(blocks),
        out_shape=pltpu.VMEM((8, 128), jnp.float32),
        cost_estimate=pl.CostEstimate(flops=1 << scale, bytes_accessed=0, transcendentals=0),
    )(*blocks)


def arrange_kernel(at_ref, *refs):
    pieces = refs[:4]
    for far, out_ref in enumerate(refs[4:]):
        for other in (0, 1):
            for t in range(4):
                start = pl.multiple_of(at_ref[t] + at_ref[4 + far] + at_ref[6 + other], 32)
                rows = [piece[pl.ds(start, 32), :] for piece in pieces]
                column = other * 512 + t * 128
                out_ref[:, column : column + 128] = jnp.concatenate(rows, axis=0).T


def arrange(at, pieces):
    whole = pl.BlockSpec(memory_space=pltpu.VMEM)
    return pl.pallas_call(
        arrange_kernel,
        in_specs=[pl.BlockSpec(memory_space=pltpu.SMEM)] + [whole] * 4,
        out_specs=[whole] * 2,
        out_shape=[pltpu.VMEM((512, 1024), jnp.bfloat16)] * 2,
        compiler_params=PARAMS,
        cost_estimate=pl.CostEstimate(flops=0, bytes_accessed=4 << 20, transcendentals=0),
    )(at, *pieces)


def near_kernel(x_ref, own_ref, other_ref, first_ref, second_ref, out_ref):
    del first_ref, second_ref
    out_ref[...] = jnp.dot(
        x_ref[:, 0:512], own_ref[...], preferred_element_type=jnp.float32
    ) + jnp.dot(x_ref[:, 512:1024], other_ref[...], preferred_element_type=jnp.float32)


def across(value):
    part = value[:, 0:128]
    for k in range(1, COLS // 128):
        part = part + value[:, k * 128 : (k + 1) * 128]
    return part


def gather_rows(step, part, acc_ref, row_ref):
    @pl.when(step == 0)
    def _():
        acc_ref[...] = part

    @pl.when(step > 0)
    def _():
        acc_ref[...] += part

    @pl.when(step == pl.num_programs(0) - 1)
    def _():
        row_ref[...] = jnp.sum(acc_ref[...].T, axis=0, keepdims=True)


def far_kernel(x_ref, *refs):
    blocks, (near_ref, out_ref, col_ref, row_ref, acc_ref) = refs[:8], refs[8:]
    value = near_ref[...]
    for half in (0, 1):
        g = jnp.concatenate([ref[...] for ref in blocks[4 * half : 4 * half + 4]], axis=0)
        x = x_ref[:, 512 * half : 512 * half + 512]
        value += jnp.dot(x, g, preferred_element_type=jnp.float32)
    out_ref[...] = value
    squares = value * value + 1e-30
    col_ref[...] = jnp.sum(squares, axis=0, keepdims=True)
    gather_rows(pl.program_id(0), across(squares), acc_ref, row_ref)


def fixed(*shape):
    return pl.BlockSpec(shape, lambda j: (0, 0))


def moving(rows):
    return pl.BlockSpec((rows, COLS), lambda j: (0, j))


def in_vmem(value):
    return pltpu.with_memory_space_constraint(value, pltpu.VMEM)


G_SPEC = moving(512)
PARAMS = pltpu.CompilerParams(vmem_limit_bytes=VMEM_LIMIT)


COST = pl.CostEstimate(flops=2 * 512 * 1024 * 2048, bytes_accessed=9 << 20, transcendentals=0)


def near_product(x, own, other, tokens):
    return pl.pallas_call(
        near_kernel,
        grid=(2048 // COLS,),
        in_specs=[fixed(512, 1024), moving(512), moving(512), fixed(8, 128), fixed(8, 128)],
        out_specs=G_SPEC,
        out_shape=jax.ShapeDtypeStruct((512, 2048), jnp.float32),
        compiler_params=PARAMS,
        cost_estimate=COST,
    )(in_vmem(x), own, other, *tokens)


def far_product(x, blocks, near):
    return pl.pallas_call(
        far_kernel,
        grid=(2048 // COLS,),
        in_specs=[fixed(512, 1024)] + [moving(128)] * 8 + [G_SPEC],
        out_specs=[G_SPEC, moving(1), fixed(1, 512)],
        out_shape=[
            pltpu.VMEM((512, 2048), jnp.float32),
            jax.ShapeDtypeStruct((1, 2048), jnp.float32),
            jax.ShapeDtypeStruct((1, 512), jnp.float32),
        ],
        scratch_shapes=[pltpu.VMEM((512, 128), jnp.float32)],
        compiler_params=PARAMS,
        cost_estimate=COST,
    )(in_vmem(x), *blocks, near)


def weigh_kernel(
    g_ref, moment_ref, parts_ref, row_ref, state_ref, copy_ref, out_ref, acc_ref, weighed_ref
):
    step = pl.program_id(0)
    sums = jnp.sum(parts_ref[...], axis=0, keepdims=True)
    state = 0.8 * moment_ref[...] + 0.2 * sums / D
    state_ref[...] = state
    copy_ref[...] = state
    scaled = g_ref[...] * lax.rsqrt(state)
    gather_rows(step, across(scaled * scaled), acc_ref, weighed_ref)

    @pl.when(step == pl.num_programs(0) - 1)
    def _():
        out_ref[:, 0:512] = row_ref[...]
        out_ref[:, 512:1024] = weighed_ref[...]


def weigh(g, column_moment, column_parts, row_part):
    return pl.pallas_call(
        weigh_kernel,
        grid=(2048 // COLS,),
        in_specs=[G_SPEC, moving(1), moving(16), fixed(1, 512)],
        out_specs=[moving(1), moving(1), fixed(1, 1024)],
        out_shape=[
            jax.ShapeDtypeStruct((1, 2048), jnp.float32),
            pltpu.VMEM((1, 2048), jnp.float32),
            jax.ShapeDtypeStruct((1, 1024), jnp.float32),
        ],
        scratch_shapes=[
            pltpu.VMEM((512, 128), jnp.float32),
            pltpu.VMEM((1, 512), jnp.float32),
        ],
        compiler_params=PARAMS,
        cost_estimate=pl.CostEstimate(
            flops=4 * 512 * 2048, bytes_accessed=4 << 20, transcendentals=0
        ),
    )(in_vmem(g), column_moment, column_parts, row_part)


def totals_kernel(moment_ref, parts_ref, state_ref, copy_ref, total_ref):
    sums = jnp.sum(parts_ref[...], axis=0, keepdims=True)
    state = 0.8 * moment_ref[...] + 0.2 * sums[:, 0:512] / FF
    state_ref[...] = state
    copy_ref[...] = state
    squares = jnp.sum(sums[:, 512:1024] / state)
    lane = lax.broadcasted_iota(jnp.int32, (1, 128), 1)
    total_ref[...] = jnp.where(lane == 0, squares, jnp.where(lane == 1, jnp.sum(state), 0.0))


def totals_of(row_moment, parts):
    return pl.pallas_call(
        totals_kernel,
        out_shape=[
            jax.ShapeDtypeStruct((1, 512), jnp.float32),
            pltpu.VMEM((1, 512), jnp.float32),
            jax.ShapeDtypeStruct((1, 128), jnp.float32),
        ],
        compiler_params=PARAMS,
        cost_estimate=pl.CostEstimate(flops=16384, bytes_accessed=70000, transcendentals=0),
    )(row_moment, parts)


def clip_kernel(g_ref, row_ref, col_ref, totals_ref, out_ref, mean_ref, rows_ref):
    @pl.when(pl.program_id(0) == 0)
    def _():
        rows_ref[...] = jnp.broadcast_to(lax.rsqrt(row_ref[...]), (128, 512)).T

    lane = lax.broadcasted_iota(jnp.int32, (1, 128), 1)
    totals = jnp.sum(totals_ref[...], axis=0, keepdims=True)
    total = jnp.sum(jnp.where(lane == 0, totals, 0.0), axis=1, keepdims=True)
    row_mean = jnp.sum(jnp.where(lane == 1, totals, 0.0), axis=1, keepdims=True) / D
    mean_ref[...] = row_mean
    clip_ratio = jnp.sqrt(row_mean * total / (D * FF))
    factor = jnp.sqrt(row_mean) / jnp.maximum(1.0, clip_ratio)
    columns = lax.rsqrt(col_ref[...]) * factor
    rows = rows_ref[...]
    for k in range(COLS // 128):
        piece = slice(k * 128, (k + 1) * 128)
        out_ref[:, piece] = g_ref[:, piece] * rows * columns[:, piece]


def clip(g, row_state, column_state, totals):
    return pl.pallas_call(
        clip_kernel,
        grid=(2048 // COLS,),
        in_specs=[G_SPEC, fixed(1, 512), moving(1), fixed(16, 128)],
        out_specs=[G_SPEC, fixed(1, 1)],
        out_shape=[
            jax.ShapeDtypeStruct((512, 2048), jnp.float32),
            jax.ShapeDtypeStruct((1, 1), jnp.float32),
        ],
        scratch_shapes=[pltpu.VMEM((512, 128), jnp.float32)],
        compiler_params=PARAMS,
        cost_estimate=pl.CostEstimate(
            flops=2 * 512 * 2048, bytes_accessed=8 << 20, transcendentals=0
        ),
    )(in_vmem(g), in_vmem(row_state), in_vmem(column_state), totals)


def cyclic(size, stride, shift):
    total = size * stride
    return [(j, (j + shift * stride) % total) for j in range(total)]


def flipped(total, mask):
    return [(j, j ^ mask) for j in range(total)]


def swap_cores(value):
    return lax.ppermute(value, "col", flipped(16, 1))


def swap_x(value, mask):
    return lax.ppermute(value, "dp", flipped(4, mask))


def move_y(value, shift):
    return lax.ppermute(value, "col", cyclic(4, 4, shift % 4))


def swap_row(value, mask):
    return lax.ppermute(value, "row", flipped(4, mask))


def swap_z(value):
    return lax.ppermute(value, "col", flipped(16, 2))


def copies(value, axis):
    rows = jnp.broadcast_to(value, (16,) + value.shape)
    return lax.all_to_all(rows, axis, 0, 0).reshape(16, value.shape[1])


def per_device(inputs, grad_out, row_moment, column_moment):
    me = lax.axis_index("dp")
    low = lax.axis_index("row")
    col = lax.axis_index("col")
    y, high, core = col // 4, col // 2 % 2, col % 2
    places = [low ^ ((y - t) % 4) for t in range(4)]
    starts = [(place % 2 * 2 + place // 2) * 128 for place in places]
    starts += [high * 64, (1 - high) * 64, core * 32, (1 - core) * 32]
    at = jnp.stack(starts).astype(jnp.int32)
    stage = lax.optimization_barrier

    pair = jnp.concatenate([inputs, swap_row(inputs, 2)])
    by_group = stage(jnp.transpose(grad_out, (1, 0, 2)))
    groups = [
        lax.dynamic_index_in_dim(by_group, me ^ s, 0, keepdims=False) for s in range(4)
    ]
    blocks = [groups[0]] + [swap_x(groups[s], s) for s in (1, 2, 3)]
    x0 = jnp.concatenate([pair, swap_row(pair, 1)])
    near, x0, at = stage((jnp.concatenate(blocks), x0, at))

    far = swap_z(near)
    nears = [move_y(near, t) for t in (1, 2, 3)]
    x0, x1 = stage((x0, swap_x(x0, 1)))
    x2 = swap_x(x0, 2)
    early = after(far, scale=35)
    far, early, x0, x2, *nears = stage((far, early, x0, x2, *nears))

    own = jnp.concatenate([near, *nears])
    other = swap_cores(own)
    x3 = swap_x(x0, 3)
    fars = [move_y(far, t) for t in (1, 2, 3)]
    x_near, x_far = arrange(at, (x0, x1, x2, x3))
    late = after(x_far, *fars, scale=35)
    late, x_near, x_far, far, *fars = stage((late, x_near, x_far, far, *fars))

    fars = [far, *fars]
    others = [swap_cores(block) for block in fars]
    gradient = near_product(x_near, own, other, (early, late))
    gradient, column_part, row_part = far_product(x_far, fars + others, gradient)
    column_state, columns, sums = weigh(
        gradient, column_moment[None], copies(column_part, "col"), row_part
    )
    row_state, rows, totals = totals_of(row_moment[None], copies(sums, ("dp", "row")))
    update, row_mean = clip(gradient, rows, columns, copies(totals, "col"))
    return (update, row_state[0], column_state[0], row_mean[0, 0])


def solution(mesh):
    return jax.shard_map(
        per_device,
        mesh=mesh,
        in_specs=(
            P(("dp", "row"), "col"),
            P(("dp", "col"), None, "row"),
            P("col"),
            P(("dp", "row")),
        ),
        out_specs=(P("col", ("dp", "row")), P("col"), P(("dp", "row")), P()),
        check_vma=False,
    )
```
